32 devices in a mesh: runs: 2 (over y), cuts: 4 (over z), event: 4 (over x, core).
Axes of the slice: x: 2, y: 2, z: 4, core: 2. Of those that a mesh axis runs over, the one named last changes fastest.
Arguments:
- partials: float32 [4, 2, 262144], P('event', None, ('runs', 'cuts')), parts along dimension 2
- coords: float32 [3, 262144], P(None, ('runs', 'cuts')), parts along dimension 1, may hold values from 0 to 800
- volume: float32 [262144], P(('runs', 'cuts')), parts along dimension 0, may hold values from 0.5 to 4
- send_blocks: int32 [8, 4, 4, 64], P(('runs', 'cuts'), 'event'), parts along dimension 0, may hold values from 0 to 255
- halo_counts: int32 [8, 4, 4], P(('runs', 'cuts'), 'event'), parts along dimension 0, may hold values from 16 to 64
- source_slots: int32 [8, 4, 64, 16], P(('runs', 'cuts'), 'event'), parts along dimension 0, may hold values from 0 to 511, as said below
- source_counts: int32 [8, 4, 64], P(('runs', 'cuts'), 'event'), parts along dimension 0, may hold values from 8 to 16
Outputs:
- smoothed: float32 [2, 262144], P(None, ('runs', 'cuts', 'event')), parts along dimension 1
The draws below stay inside these ranges and needn't reach their ends.
There are 2 independent parts, one for each index of `runs`. The reference program is written for one: setup_inputs(seed, part) draws one part's arguments, and reference() takes and returns one part's arrays. A program takes and returns all parts, laid end to end along the dimension named above; each array names one. Nothing has to cross between parts.
Inputs may be any that keep to these rules, and one draw needn't show every extreme that they name: `source_slots`: slot 0 of target block t of owner (c, e) is its own block, e * 64 + t; every slot names a block of the own slice or a halo slot.
All inputs are finite; a program needn't handle non-finite values.
Results may differ from the reference program's by a relative error of at most 0.00019.
Values sent between devices are 32-bit elements; how exact they have to be, the bound alone decides.
No kernel may reach another device: no remote copies, remote signals or barrier semaphores. Data moves between devices by JAX's collectives and lax.ppermute only.
A program may use at most 64 MiB of HBM per device.

```python
import math
import jax
import jax.numpy as jnp
from jax import lax

BLOCK = 128
NBO = 64
CAP = 64
LIST = 16
NBS = 256
POINTS = 131072
GRID = 1
N_CUTS = 4
N_EVENT = 4


def halo_plan(key):
    plan_key = jax.random.fold_in(key, 101)
    count_key, region_key, pick_key, offset_key = jax.random.split(plan_key, 4)
    lowest = max(1, CAP // 4)
    counts = jax.random.randint(count_key, (N_CUTS, N_EVENT, 4), lowest, CAP + 1).astype(jnp.int32)
    counts = counts.at[0, 0, 0].set(lowest).at[0, 0, 3].set(CAP)
    shape = (N_CUTS, N_EVENT, NBO, LIST)
    region = jax.random.randint(region_key, shape, 0, 8).astype(jnp.int32)
    own_pick = jax.random.randint(pick_key, shape, 0, NBS).astype(jnp.int32)
    raw_offset = jax.random.randint(offset_key, shape, 0, CAP).astype(jnp.int32)
    direction = jnp.clip(region - 4, 0, 3)
    halo_slot = NBS + direction * CAP + raw_offset
    slot_table = jnp.where(region < 4, own_pick, halo_slot)
    own_block = jnp.broadcast_to(jnp.arange(N_EVENT, dtype=jnp.int32)[None, :, None] * NBO + jnp.arange(NBO, dtype=jnp.int32)[None, None, :], (N_CUTS, N_EVENT, NBO))
    slot_table = slot_table.at[:, :, :, 0].set(own_block)
    slot_table = slot_table.at[0, 0, 0, 1].set(0).at[0, 0, 0, LIST - 1].set(NBS + 4 * CAP - 1)
    return (counts, slot_table)


def draw_halo_counts(key, part):
    counts, slot_table = halo_plan(key)
    return counts


def draw_source_slots(key, part):
    counts, slot_table = halo_plan(key)
    return slot_table


def draw_partials(key, part):
    key = jax.random.fold_in(key, 7)
    mean_key, noise_key = jax.random.split(key)
    block_count = POINTS // BLOCK
    means = jax.random.uniform(mean_key, (N_EVENT, 2, block_count, 1), jnp.float32, -1.2, 1.2)
    noise = jax.random.normal(noise_key, (N_EVENT, 2, block_count, BLOCK), jnp.float32) * 0.5
    return (means + noise).reshape(N_EVENT, 2, POINTS)


def with_ends(values, rng, low, top_value):
    place = [jax.random.randint(jax.random.fold_in(rng, axis), (), 0, length) for axis, length in enumerate(values.shape)]
    main_axis = values.shape.index(max(values.shape))
    next_to = place[:main_axis] + [(place[main_axis] + 1) % values.shape[main_axis]] + place[main_axis + 1:]
    return values.at[tuple(place)].set(low).at[tuple(next_to)].set(top_value)


def level_of(stream_key, extent, shards, low, high):
    factor_of = 1.0
    for axis_at, parts in shards:
        draws = jax.random.uniform(jax.random.fold_in(jax.random.fold_in(stream_key, 6), axis_at), (parts,), jnp.float32, low / len(shards), high / len(shards))
        factor_of = factor_of * jnp.repeat(jnp.exp(draws), extent[axis_at] // parts).reshape((-1,) + (1,) * (len(extent) - 1 - axis_at))
    return factor_of


def setup_inputs(seed: int = 0, part: int = 0) -> dict:
    seeds = jax.random.split(jax.random.key(seed), 8)
    own_keys = jax.random.split(jax.random.fold_in(seeds[7], part), 8)
    partials = draw_partials(jax.random.fold_in(jax.random.fold_in(seeds[7], part), 71), part)
    coords = jnp.clip(800.0 * jax.random.uniform(own_keys[1], (3, POINTS), jnp.float32) ** level_of(own_keys[1], (3, POINTS), ((1, 4),), -0.2, 0.2), 0.0, 800.0)
    volume = jnp.clip(jnp.exp(math.log(4.0) - 2.0794415 * jax.random.uniform(own_keys[2], (POINTS,), jnp.float32) ** level_of(own_keys[2], (POINTS,), ((0, 4),), -0.2, 0.2)), 0.5, 4.0)
    send_blocks = with_ends(jax.random.randint(own_keys[3], (N_CUTS, N_EVENT, 4, CAP), 0, NBS), jax.random.fold_in(own_keys[3], 1), 0, NBS - 1).astype(jnp.int32)
    halo_counts = draw_halo_counts(jax.random.fold_in(jax.random.fold_in(seeds[7], part), 71), part)
    source_slots = draw_source_slots(jax.random.fold_in(jax.random.fold_in(seeds[7], part), 71), part)
    source_counts = with_ends(jax.random.randint(own_keys[6], (N_CUTS, N_EVENT, NBO), LIST // 2, LIST + 1), jax.random.fold_in(own_keys[6], 1), LIST // 2, LIST).astype(jnp.int32)
    return dict(partials=partials, coords=coords, volume=volume, send_blocks=send_blocks, halo_counts=halo_counts, source_slots=source_slots, source_counts=source_counts)


sigma_km = 50.0


def smooth_group(targets, sources, live_mask):
    distance = jnp.zeros((targets.shape[1], targets.shape[2], sources.shape[2], sources.shape[3]), jnp.float32)
    for coord_row in range(3):
        offset_gap = targets[coord_row][:, :, None, None] - sources[coord_row][:, None, :, :]
        distance = distance + offset_gap * offset_gap
    weights = jnp.exp(distance * (-0.5 / (sigma_km * sigma_km))) * live_mask[:, None, :, None]
    totals = jnp.einsum("gtls,cgls->cgt", weights, sources[3:6], precision=lax.Precision.HIGHEST)
    return totals[1:3] / totals[0]


def reference(partials, coords, volume, send_blocks, halo_counts, source_slots, source_counts):
    summed = jnp.sum(partials, axis=0)
    slab_table = jnp.concatenate([coords, volume[None], volume[None] * summed], axis=0)
    slab_table = slab_table.reshape(6, N_CUTS * NBS, BLOCK)
    offsets = jnp.array([1, -1, GRID, -GRID], jnp.int32)
    cut_ids = jnp.arange(N_CUTS, dtype=jnp.int32)[:, None, None]
    event_ids = jnp.broadcast_to(jnp.arange(N_EVENT, dtype=jnp.int32)[None, :, None], (N_CUTS, N_EVENT, 4))
    direction_ids = jnp.broadcast_to(jnp.arange(4, dtype=jnp.int32)[None, None, :], (N_CUTS, N_EVENT, 4))
    senders = jnp.broadcast_to((cut_ids - offsets[None, None, :]) % N_CUTS, (N_CUTS, N_EVENT, 4))
    sent_blocks = send_blocks[senders, event_ids, direction_ids]
    halo_ids = (senders[..., None] * NBS + sent_blocks).reshape(N_CUTS, N_EVENT, 4 * CAP)
    own_ids = jnp.broadcast_to(cut_ids * NBS + jnp.arange(NBS, dtype=jnp.int32)[None, None, :], (N_CUTS, N_EVENT, NBS))
    pool_ids = jnp.concatenate([own_ids, halo_ids], axis=2)
    halo_live = (jnp.arange(CAP, dtype=jnp.int32)[None, None, None, :] < halo_counts[..., None]).astype(jnp.float32)
    pool_live = jnp.concatenate([jnp.ones((N_CUTS, N_EVENT, NBS), jnp.float32), halo_live.reshape(N_CUTS, N_EVENT, 4 * CAP)], axis=2)
    flat_slots = source_slots.reshape(N_CUTS, N_EVENT, NBO * LIST)
    slot_ids = jnp.take_along_axis(pool_ids, flat_slots, axis=2).reshape(N_CUTS, N_EVENT, NBO, LIST)
    slot_live = jnp.take_along_axis(pool_live, flat_slots, axis=2).reshape(N_CUTS, N_EVENT, NBO, LIST)
    used = (jnp.arange(LIST, dtype=jnp.int32)[None, None, None, :] < source_counts[..., None]).astype(jnp.float32)
    slot_live = slot_live * used
    target_ids = (jnp.arange(N_CUTS, dtype=jnp.int32)[:, None, None] * NBS
                  + jnp.arange(N_EVENT, dtype=jnp.int32)[None, :, None] * NBO
                  + jnp.arange(NBO, dtype=jnp.int32)[None, None, :])

    def one_group(group_items):
        target_group, slot_group, live_group = group_items
        targets = jnp.take(slab_table, target_group, axis=1)
        sources = jnp.take(slab_table, slot_group.reshape(-1), axis=1).reshape(6, 4, LIST, BLOCK)
        return smooth_group(targets, sources, live_group)

    results = lax.map(one_group, (target_ids.reshape(-1, 4), slot_ids.reshape(-1, 4, LIST), slot_live.reshape(-1, 4, LIST)))
    return results.transpose(1, 0, 2, 3).reshape(2, POINTS)
```

```python
import functools
import math

import jax
import jax.numpy as jnp
from jax import lax
from jax.experimental import pallas as pl
from jax.experimental.pallas import tpu as pltpu
from jax.sharding import PartitionSpec as P

BLOCK = 128
FEATURES = 48
PAIRS = 16
CODE = 1024
sigma_km = 50.0
centre_km = 400.0
scale = math.sqrt(math.log2(math.e)) / sigma_km

f32 = jnp.float32
bf16 = jnp.bfloat16
i32 = jnp.int32


def vmem():
    return pl.BlockSpec(memory_space=pltpu.VMEM)


def smem():
    return pl.BlockSpec(memory_space=pltpu.SMEM)


def params(mib):
    return pltpu.CompilerParams(vmem_limit_bytes=mib << 20)


def shifted(block, axis, distance):
    devices = range(lax.axis_size(axis))
    route = [((i - distance) % len(devices), i) for i in devices]
    return lax.ppermute(block, axis, route)


def crossed(block, axis, bit):
    route = [(i ^ bit, i) for i in range(lax.axis_size(axis))]
    return lax.ppermute(block, axis, route)


def split(values):
    high = values.astype(bf16).astype(f32)
    rest = values - high
    middle = rest.astype(bf16).astype(f32)
    return high, middle, rest - middle


def feature_rows(x, y, z, fourth, fifth):
    row = lax.broadcasted_iota(i32, (8, BLOCK), 0)
    rows = jnp.where(row == 3, fourth, jnp.where(row == 4, fifth, 0.0))
    rows = jnp.where(row == 2, z, rows)
    rows = jnp.where(row == 1, y, rows)
    return jnp.where(row == 0, x, rows)


def target_features(x, y, z):
    x, y, z = [(c - centre_km) * scale for c in (x, y, z)]
    norm = -0.5 * (x * x + y * y + z * z)
    high, middle, low = split(feature_rows(x, y, z, 1.0, norm))
    return jnp.concatenate([high, middle, low, high, middle, high], axis=0).astype(bf16)


def source_features(x, y, z, volume):
    x, y, z = [(c - centre_km) * scale for c in (x, y, z)]
    norm = -0.5 * (x * x + y * y + z * z)
    high, middle, low = split(feature_rows(x, y, z, norm + jnp.log2(volume), 1.0))
    return jnp.concatenate([high, high, high, middle, middle, low], axis=0)


def own_features_kernel(event_ref, coords_ref, volume_ref, source_ref, target_ref):
    block_total = volume_ref.shape[0]
    own_blocks = target_ref.shape[0]

    def coords_of(b):
        at = pl.ds(pl.multiple_of(b * BLOCK, BLOCK), BLOCK)
        return [coords_ref[r : r + 1, at] for r in range(3)]

    def one_source(b, _):
        rows = source_features(*coords_of(b), volume_ref[pl.ds(b, 1), :])
        source_ref[b] = rows.T.astype(bf16)
        return 0

    def one_target(t, _):
        target_ref[t] = target_features(*coords_of(event_ref[0] * own_blocks + t))
        return 0

    lax.fori_loop(0, block_total, one_source, 0, unroll=8)
    lax.fori_loop(0, own_blocks, one_target, 0, unroll=8)
    column = lax.broadcasted_iota(i32, (BLOCK, FEATURES), 1)
    source_ref[block_total] = jnp.where(column == 3, -10000.0, 0.0).astype(bf16)


def own_features(event, coords, volume, own_blocks):
    block_total = volume.shape[0]
    return pl.pallas_call(
        own_features_kernel,
        out_shape=(
            pltpu.VMEM((block_total + 1, BLOCK, FEATURES), bf16),
            pltpu.VMEM((own_blocks, FEATURES, BLOCK), bf16),
        ),
        in_specs=[smem(), vmem(), vmem()],
        out_specs=(vmem(), vmem()),
        compiler_params=params(8),
        cost_estimate=pl.CostEstimate(flops=6000000, bytes_accessed=6000000, transcendentals=0),
        name="own_features",
    )(event, coords, volume)


def halo_features_kernel(*refs):
    *given, target_ref = refs
    own_blocks = target_ref.shape[0] // len(given)
    for s, ref in enumerate(given):

        def one_target(t, _):
            rows = [ref[pl.ds(r * own_blocks + t, 1), :] for r in range(3)]
            target_ref[s * own_blocks + t] = target_features(*rows)
            return 0

        lax.fori_loop(0, own_blocks, one_target, 0, unroll=8)


def halo_features(given, own_blocks):
    return pl.pallas_call(
        halo_features_kernel,
        out_shape=pltpu.VMEM((len(given) * own_blocks, FEATURES, BLOCK), bf16),
        in_specs=[vmem()] * len(given),
        out_specs=vmem(),
        compiler_params=params(8),
        cost_estimate=pl.CostEstimate(flops=2000000, bytes_accessed=2000000, transcendentals=0),
        name="halo_features",
    )(*given)


def value_rows(first, second):
    row = lax.broadcasted_iota(i32, (8, BLOCK), 0)
    both = jnp.where((row & 1) == 1, first, second)
    high, middle, low = split(both)
    rows = jnp.where(row < 5, jnp.where(row < 3, high, middle), jnp.where(row < 7, low, 0.0))
    rows = jnp.where(row == 0, 1.0, rows).astype(bf16)
    return jnp.concatenate([rows, rows], axis=1)


def values_kernel(order_ref, *refs):
    *given, value_ref = refs
    piece_blocks = given[0].shape[1] // BLOCK
    for piece, ref in enumerate(given):
        start = order_ref[piece] * piece_blocks

        def one_block(b, _):
            at = pl.ds(pl.multiple_of(b * BLOCK, BLOCK), BLOCK)
            value_ref[start + b] = value_rows(ref[0:1, at], ref[1:2, at])
            return 0

        lax.fori_loop(0, piece_blocks, one_block, 0, unroll=8)
    value_ref[value_ref.shape[0] - 1] = jnp.zeros((8, 2 * BLOCK), bf16)


def values_table(order, given, block_total):
    return pl.pallas_call(
        values_kernel,
        out_shape=pltpu.VMEM((block_total + 1, 8, 2 * BLOCK), bf16),
        in_specs=[smem()] + [vmem()] * len(given),
        out_specs=vmem(),
        compiler_params=params(8),
        cost_estimate=pl.CostEstimate(flops=1000000, bytes_accessed=1000000, transcendentals=0),
        name="values_table",
    )(order, *given)


def totals_kernel(
    sets, own_blocks, steps_ref, list_ref, block_ref, source_ref, target_ref, value_ref, out_ref,
    sum_ref, weight_ref,
):
    chunks = PAIRS // 2
    total_steps = steps_ref[0]
    for s in range(1, sets):
        total_steps = total_steps + steps_ref[s]

    def pair(s, k, i):
        code = list_ref[s, k * PAIRS + i]
        block = code & (CODE - 1)
        if block_ref is not None:
            block = block_ref[block]
        return s * own_blocks + (code >> 10), block

    def following(s, k):
        ends = k + 1 >= steps_ref[s]
        after = jnp.minimum(jnp.where(ends, s + 1, s), sets - 1)
        return after, jnp.where(ends, 0, k + 1)

    def make(s, k, c):
        for h in range(2):
            t, b = pair(s, k, 2 * c + h)
            at = slice(h * BLOCK, (h + 1) * BLOCK)
            weight = jnp.exp2(jnp.dot(source_ref[b], target_ref[t], preferred_element_type=f32))
            high = weight.astype(bf16)
            weight_ref[c, 0:BLOCK, at] = high
            weight_ref[c, BLOCK : 2 * BLOCK, at] = (weight - high.astype(f32)).astype(bf16)

    def use(s, k, c):
        t0, b0 = pair(s, k, 2 * c)
        t1, b1 = pair(s, k, 2 * c + 1)
        values = jnp.concatenate([value_ref[b0], value_ref[b1]], axis=0)
        sums = jnp.dot(values, weight_ref[c], preferred_element_type=f32)
        sum_ref[pl.ds(pl.multiple_of(t0 * 8, 8), 8), :] += sums[0:8, 0:BLOCK]
        sum_ref[pl.ds(pl.multiple_of(t1 * 8, 8), 8), :] += sums[8:16, BLOCK : 2 * BLOCK]

    sum_ref[...] = jnp.zeros(sum_ref.shape, f32)
    zero = jnp.int32(0)
    for c in range(chunks):
        make(zero, zero, c)

    def step(_, at):
        s, k = at
        s_next, k_next = following(s, k)
        for c in range(chunks):
            use(s, k, c)
            make(s_next, k_next, c)
        return s_next, k_next

    lax.fori_loop(0, total_steps, step, (zero, zero))

    for s in range(sets):
        rows = [
            sum_ref[pl.ds(s * own_blocks * 8 + r, own_blocks, stride=8), :] for r in range(7)
        ]
        out_ref[s, 0] = rows[0]
        out_ref[s, 1] = rows[1] + rows[3] + rows[5]
        out_ref[s, 2] = rows[2] + rows[4] + rows[6]


def totals_of(name, steps, lists, blocks, sources, targets, values, own_blocks):
    sets = lists.shape[0]
    kernel = functools.partial(totals_kernel, sets, own_blocks)
    given = [steps, lists, blocks, sources, targets, values]
    specs = [smem(), smem(), smem(), vmem(), vmem(), vmem()]
    if blocks is None:
        del given[2], specs[2]
        inner = kernel
        kernel = lambda steps_ref, list_ref, *rest: inner(steps_ref, list_ref, None, *rest)
    return pl.pallas_call(
        kernel,
        out_shape=jax.ShapeDtypeStruct((sets, 3, own_blocks, BLOCK), f32),
        in_specs=specs,
        out_specs=vmem(),
        scratch_shapes=[
            pltpu.VMEM((sets * own_blocks * 8, BLOCK), f32),
            pltpu.VMEM((PAIRS // 2, 2 * BLOCK, 2 * BLOCK), bf16),
        ],
        compiler_params=params(12),
        cost_estimate=pl.CostEstimate(
            flops=400000000, bytes_accessed=4000000, transcendentals=8000000
        ),
        name=name,
    )(*given)


def compact(live, code, spare):
    places = live.shape[1]
    live = live.astype(i32)
    before = jnp.tril(jnp.ones((places, places), i32), -1)
    position = jnp.sum(live[:, None, :] * before[None], axis=2)
    position = jnp.where(live == 1, position, places)
    hit = position[:, None, :] == jnp.arange(places, dtype=i32)[None, :, None]
    flat = spare + jnp.sum(jnp.where(hit, (code - spare)[:, None, :], 0), axis=2)
    count = jnp.sum(live, axis=1)
    return flat, jnp.maximum((count + PAIRS - 1) // PAIRS, 1)


def local(partials, coords, volume, send_blocks, halo_counts, source_slots, source_counts):
    cut_count = lax.axis_size("cuts")
    event_count = lax.axis_size("event")
    block_total = volume.shape[0] // BLOCK
    own_blocks = source_slots.shape[2]
    list_width = source_slots.shape[3]
    capacity = send_blocks.shape[3]
    grid_step = cut_count // 4
    my_event = lax.axis_index("event")

    groups = {}
    for k, offset in enumerate((1, -1, grid_step, -grid_step)):
        groups.setdefault(offset % cut_count, []).append(k)

    slots = source_slots[0, 0]
    used = jnp.arange(list_width, dtype=i32)[None, :] < source_counts[0, 0][:, None]
    relative = slots - block_total
    direction = relative // capacity
    limit = jnp.zeros_like(slots)
    for k in range(4):
        limit = jnp.where(direction == k, halo_counts[0, 0, k], limit)
    halo_live = used & (relative >= 0) & (relative % capacity < limit)
    target_code = jnp.arange(own_blocks, dtype=i32)[:, None] * CODE
    lives = [used & (relative < 0)]
    codes = [target_code + slots]
    for members in groups.values():
        chosen = functools.reduce(jnp.logical_or, [direction == k for k in members])
        lives.append(halo_live & chosen)
        codes.append(target_code + relative)
    places = own_blocks * list_width
    spare = jnp.array([block_total] + [4 * capacity] * len(groups), i32)[:, None]
    lists, steps = compact(
        jnp.stack(lives).reshape(-1, places), jnp.stack(codes).reshape(-1, places), spare
    )

    own_at = my_event * own_blocks * BLOCK
    own_coords = lax.dynamic_slice_in_dim(coords, own_at, own_blocks * BLOCK, axis=1)
    own_coords = own_coords.reshape(3 * own_blocks, BLOCK)
    arrived = []
    for s, offset in enumerate(groups):
        listed = lists[s + 1].astype(f32).reshape(-1, BLOCK)
        step_rows = jnp.broadcast_to(steps[s + 1].astype(f32), (8, BLOCK))
        parcel = jnp.concatenate([own_coords, listed, step_rows], axis=0)
        arrived.append(shifted(parcel, "cuts", -offset))

    mine = partials[0]
    if event_count == 4:
        half = mine.shape[1] // 2
        core = my_event & 1
        chip = mine + crossed(mine, "event", 1)
        part = lax.dynamic_slice_in_dim(chip, core * half, half, axis=1)
        part = part + crossed(part, "event", 2)
        other = crossed(part, "event", 1)
        summed = [part, other]
        order = jnp.stack([core, 1 - core])
    else:
        summed = [lax.psum(mine, "event")]
        order = jnp.zeros((1,), i32)

    sources, targets = own_features(
        my_event.reshape(1), coords, volume.reshape(block_total, BLOCK), own_blocks
    )
    head = 3 * own_blocks
    tail = head + places // BLOCK
    halo_targets = halo_features(arrived, own_blocks)
    halo_lists = jnp.stack([a[head:tail].reshape(places) for a in arrived]).astype(i32)
    halo_steps = jnp.stack([a[tail, 0] for a in arrived]).astype(i32)
    sent = jnp.concatenate([send_blocks[0, 0].reshape(-1), jnp.full((8,), block_total, i32)])

    values = values_table(order, summed, block_total)
    halo_totals = totals_of(
        "halo_totals", halo_steps, halo_lists, sent, sources, halo_targets, values, own_blocks
    )
    returned = [
        shifted(halo_totals[s], "cuts", offset) for s, offset in enumerate(groups)
    ]
    own_totals = totals_of(
        "own_totals", steps[:1], lists[:1], None, sources, targets, values, own_blocks
    )
    totals = own_totals[0]
    for part in returned:
        totals = totals + part
    return (totals[1:3] / totals[0]).reshape(2, own_blocks * BLOCK)


def solution(mesh):
    placed = (
        P("event", None, ("runs", "cuts")),
        P(None, ("runs", "cuts")),
        P(("runs", "cuts")),
        P(("runs", "cuts"), "event", None, None),
        P(("runs", "cuts"), "event", None),
        P(("runs", "cuts"), "event", None, None),
        P(("runs", "cuts"), "event", None),
    )
    return jax.shard_map(
        local,
        mesh=mesh,
        in_specs=placed,
        out_specs=P(None, ("runs", "cuts", "event")),
        check_vma=False,
    )
```

```python
import functools
import math

import jax
import jax.numpy as jnp
from jax import lax
from jax.experimental import pallas as pl
from jax.experimental.pallas import tpu as pltpu
from jax.sharding import PartitionSpec as P

BLOCK = 128
FEATURES = 48
PAIR_BITS = 5
PAIRS = 1 << PAIR_BITS
CODE = 1024
sigma_km = 50.0
centre_km = 400.0
scale = math.sqrt(math.log2(math.e)) / sigma_km

f32 = jnp.float32
bf16 = jnp.bfloat16
i32 = jnp.int32


def vmem():
    return pl.BlockSpec(memory_space=pltpu.VMEM)


def smem():
    return pl.BlockSpec(memory_space=pltpu.SMEM)


def held(*arrays):
    return [pltpu.with_memory_space_constraint(a, pltpu.VMEM) for a in arrays]


def far(*arrays):
    return [pltpu.with_memory_space_constraint(a, pltpu.HBM) for a in arrays]


def lasting(microseconds):
    flops = int(microseconds * 1.15e9)
    return pl.CostEstimate(flops=flops, bytes_accessed=1000000, transcendentals=0)


def params(mib):
    return pltpu.CompilerParams(vmem_limit_bytes=mib << 20)


def swapped(block, stride, turn):
    devices = lax.axis_size("cuts")
    step = [stride, -stride] if turn == 0 else [-stride, stride]
    route = [(i, (i + step[(i // stride) % 2]) % devices) for i in range(devices)]
    return lax.ppermute(block, "cuts", route)


def crossed(block, axis, bit):
    route = [(i ^ bit, i) for i in range(lax.axis_size(axis))]
    return lax.ppermute(block, axis, route)


def split(values):
    high = values.astype(bf16).astype(f32)
    rest = values - high
    middle = rest.astype(bf16).astype(f32)
    return high, middle, rest - middle


def feature_rows(offsets, fourth, fifth):
    row = lax.broadcasted_iota(i32, (8, BLOCK), 0)
    rows = jnp.where(row == 3, fourth, jnp.where(row == 4, fifth, 0.0))
    return jnp.where(row < 3, offsets, rows)


def place(coords_ref, pad_ref, slot, b):
    at = pl.ds(pl.multiple_of(b * BLOCK, BLOCK), BLOCK)
    pad_ref[slot, 0:3, :] = (coords_ref[:, at] - centre_km) * scale
    offsets = pad_ref[slot]
    return offsets, -0.5 * jnp.sum(offsets * offsets, axis=0, keepdims=True)


def target_features(offsets, norm):
    high, middle, low = split(feature_rows(offsets, 1.0, norm))
    return jnp.concatenate([high, middle, low, high, middle, high], axis=0).astype(bf16)


def own_features_kernel(event_ref, coords_ref, volume_ref, source_ref, target_ref, pad_ref, log_ref):
    block_total = volume_ref.shape[0]
    own_blocks = target_ref.shape[0]
    slots = pad_ref.shape[0]
    pad_ref[...] = jnp.zeros(pad_ref.shape, f32)
    log_ref[...] = jnp.log2(volume_ref[...])

    def some_sources(n, _):
        for slot in range(slots):
            b = n * slots + slot
            offsets, norm = place(coords_ref, pad_ref, slot, b)
            high, middle, low = split(feature_rows(offsets, norm + log_ref[pl.ds(b, 1), :], 1.0))
            rows = jnp.concatenate([high, high, high, middle, middle, low], axis=0)
            source_ref[b] = rows.T.astype(bf16)
        return 0

    def some_targets(n, _):
        for slot in range(slots):
            t = n * slots + slot
            block = event_ref[0] * own_blocks + t
            target_ref[t] = target_features(*place(coords_ref, pad_ref, slot, block))
        return 0

    lax.fori_loop(0, block_total // slots, some_sources, 0)
    lax.fori_loop(0, own_blocks // slots, some_targets, 0)
    column = lax.broadcasted_iota(i32, (BLOCK, FEATURES), 1)
    source_ref[block_total] = jnp.where(column == 3, -10000.0, 0.0).astype(bf16)


def own_features(event, coords, volume, own_blocks):
    block_total = volume.shape[0]
    return pl.pallas_call(
        own_features_kernel,
        out_shape=(
            pltpu.VMEM((block_total + 1, BLOCK, FEATURES), bf16),
            pltpu.VMEM((own_blocks, FEATURES, BLOCK), bf16),
        ),
        in_specs=[smem(), vmem(), vmem()],
        out_specs=(vmem(), vmem()),
        scratch_shapes=[pltpu.VMEM((16, 8, BLOCK), f32), pltpu.VMEM((block_total, BLOCK), f32)],
        compiler_params=params(8),
        cost_estimate=lasting(4),
        name="own_features",
    )(event, *held(coords, volume))


def prepare_kernel(
    strides, capacity, event_ref, cut_ref, halo_given, slot_given, count_given, coords_given, volume_given,
    coords_ref, volume_ref, own_ref, *refs,
):
    parcels, rest = refs[: 2 * len(strides)], refs[2 * len(strides) :]
    halo_ref, slot_ref, count_ref, row_ref, arrival = rest
    width, own_blocks = slot_ref.shape
    block_total = volume_ref.shape[0]
    sets = len(parcels) + 1
    brought = [
        (halo_given, halo_ref), (slot_given, slot_ref), (count_given, count_ref),
        (coords_given, coords_ref), (volume_given, volume_ref),
    ]
    brought = [
        pltpu.make_async_copy(given, ref, arrival.at[n]) for n, (given, ref) in enumerate(brought)
    ]
    for copy in brought:
        copy.start()
    for copy in brought[:3]:
        copy.wait()
    row_ref[...] = jnp.zeros(row_ref.shape, i32)
    row_ref[0:width, 0:own_blocks] = slot_ref[...]
    row_ref[width : width + 1, 0:own_blocks] = count_ref[...]
    shape = (width, BLOCK)
    slots = row_ref[0:width]
    used = lax.broadcasted_iota(i32, shape, 0) < row_ref[width : width + 1]
    halo = slots - block_total
    lives = [used & (halo < 0)]
    for stride, members in strides:
        both = []
        for directions in members:
            live = jnp.zeros(shape, i32)
            for k in directions:
                near = (halo >= k * capacity) & (halo - k * capacity < halo_ref[0, k])
                live = live + (near & (halo < (k + 1) * capacity)).astype(i32)
            both.append(live)
        odd = (cut_ref[0] // stride) % 2
        for first, second in (both[::-1], both):
            live = first * (1 - odd) + second * odd
            lives.append(used & (live > 0))
    rows = sets * width
    live = jnp.concatenate([l.astype(f32) for l in lives], axis=0).astype(bf16)
    near = lax.broadcasted_iota(i32, (BLOCK, BLOCK), 0)
    across = lax.broadcasted_iota(i32, (BLOCK, BLOCK), 1)
    earlier = (near < across).astype(f32).astype(bf16)
    rank = jnp.dot(live, earlier, preferred_element_type=f32)
    count = jnp.dot(live, jnp.ones((BLOCK, BLOCK), bf16), preferred_element_type=f32).astype(bf16)
    near = lax.broadcasted_iota(i32, (rows, rows), 0)
    across = lax.broadcasted_iota(i32, (rows, rows), 1)
    alike = near // width == across // width
    above = (alike & (across < near)).astype(f32).astype(bf16)
    before = jnp.dot(above, count, preferred_element_type=f32)
    total = jnp.dot(alike.astype(f32).astype(bf16), count, preferred_element_type=f32).astype(i32)
    position = (before + rank).astype(i32)
    list_rows = own_blocks * width // BLOCK
    high = jnp.full(shape, -1, i32)
    low = jnp.full(shape, -1, i32)
    for s in range(sets):
        here = position[s * width : (s + 1) * width]
        high = jnp.where(lives[s], (here >> 7) + s * list_rows, high)
        low = jnp.where(lives[s], here & (BLOCK - 1), low)
    block = jnp.where(halo < 0, slots, halo)
    target = lax.broadcasted_iota(i32, shape, 1).astype(f32)
    parts = [target, (block >> 3).astype(f32), (block & 7).astype(f32)]
    list_row = lax.broadcasted_iota(i32, (sets * list_rows, BLOCK), 0)
    list_lane = lax.broadcasted_iota(i32, (BLOCK, BLOCK), 0)
    codes, places = [], []
    for i in range(width):
        hit = list_row == high[i : i + 1, :]
        codes.append(
            jnp.concatenate([jnp.where(hit, p[i : i + 1, :], 0.0) for p in parts], axis=0)
        )
        places.append((list_lane == low[i : i + 1, :]).astype(f32).astype(bf16))
    codes = jnp.concatenate([c.astype(bf16) for c in codes], axis=1)
    places = jnp.concatenate(places, axis=1)
    found = lax.dot_general(
        codes, places, (((1,), (1,)), ((), ())), preferred_element_type=f32
    ).astype(i32)
    size = sets * list_rows
    found = found[0:size] * CODE + found[size : 2 * size] * 8 + found[2 * size : 3 * size]
    entry = lax.broadcasted_iota(i32, (list_rows, BLOCK), 0) * BLOCK
    entry = entry + lax.broadcasted_iota(i32, (list_rows, BLOCK), 1)
    for s in range(sets):
        count = total[s * width : s * width + 8]
        spare = block_total if s == 0 else 4 * capacity
        listed = jnp.where(entry < count[0:list_rows], found[s * list_rows : (s + 1) * list_rows], spare)
        steps = jnp.maximum((count + PAIRS - 1) >> PAIR_BITS, 1)
        if s == 0:
            own_ref[0, 0:list_rows] = listed
            own_ref[0, list_rows : list_rows + 8] = steps
        else:
            parcels[s - 1][3 * own_blocks : 3 * own_blocks + list_rows] = listed.astype(f32)
            parcels[s - 1][3 * own_blocks + list_rows :] = steps.astype(f32)

    for copy in brought[3:]:
        copy.wait()

    def some_coords(t, _):
        at = pl.multiple_of((event_ref[0] * own_blocks + t) * BLOCK, BLOCK)
        given = coords_ref[:, pl.ds(at, BLOCK)]
        for parcel in parcels:
            for r in range(3):
                parcel[pl.ds(r * own_blocks + t, 1), :] = given[r : r + 1]
        return 0

    lax.fori_loop(0, own_blocks, some_coords, 0, unroll=8)


def prepare(strides, capacity, event, cut, halo_counts, slots, counts, coords, volume):
    width, own_blocks = slots.shape
    list_rows = own_blocks * width // BLOCK
    parcel = jax.ShapeDtypeStruct((3 * own_blocks + list_rows + 8, BLOCK), f32)
    return pl.pallas_call(
        functools.partial(prepare_kernel, strides, capacity),
        out_shape=(
            pltpu.VMEM(coords.shape, f32),
            pltpu.VMEM(volume.shape, f32),
            jax.ShapeDtypeStruct((1, list_rows + 8, BLOCK), i32),
        )
        + (parcel,) * (2 * len(strides)),
        in_specs=[smem()] * 2 + [pl.BlockSpec(memory_space=pltpu.HBM)] * 5,
        out_specs=(vmem(),) * (2 * len(strides) + 3),
        scratch_shapes=[
            pltpu.SMEM(halo_counts.shape, i32),
            pltpu.VMEM(slots.shape, i32),
            pltpu.VMEM(counts.shape, i32),
            pltpu.VMEM((width + 8, BLOCK), i32),
            pltpu.SemaphoreType.DMA((5,)),
        ],
        compiler_params=params(8),
        cost_estimate=lasting(2),
        name="prepare",
    )(event, cut, *far(halo_counts, slots, counts, coords, volume))


def halo_features_kernel(block_total, own_blocks, sent_ref, *refs):
    *given, target_ref, list_ref, pad_ref, row_ref = refs
    slots = pad_ref.shape[0]
    directions, capacity = sent_ref.shape
    pad_ref[...] = jnp.zeros(pad_ref.shape, f32)
    row_ref[...] = jnp.zeros(row_ref.shape, i32)
    row_ref[0:directions, 0:capacity] = sent_ref[...]
    head = 3 * own_blocks
    list_rows = list_ref.shape[1] - 8
    for s, ref in enumerate(given):
        code = ref[head : head + list_rows].astype(i32)
        slot = code & (CODE - 1)
        block = jnp.full(code.shape, block_total, i32)
        for k in range(directions):
            here = (slot >= k * capacity) & (slot < (k + 1) * capacity)
            row = jnp.broadcast_to(row_ref[k : k + 1, :], code.shape)
            at = jnp.where(here, slot - k * capacity, 0)
            block = jnp.where(here, jnp.take_along_axis(row, at, axis=1), block)
        list_ref[s, 0:list_rows] = code - slot + block
        list_ref[s, list_rows:] = ref[head + list_rows :].astype(i32)

        def some_targets(n, _):
            for q in range(slots):
                t = n * slots + q
                for r in range(3):
                    row = ref[pl.ds(r * own_blocks + t, 1), :]
                    pad_ref[q, r : r + 1, :] = (row - centre_km) * scale
                offsets = pad_ref[q]
                norm = -0.5 * jnp.sum(offsets * offsets, axis=0, keepdims=True)
                target_ref[s * own_blocks + t] = target_features(offsets, norm)
            return 0

        lax.fori_loop(0, own_blocks // slots, some_targets, 0)


def halo_features(sent, given, block_total, own_blocks):
    list_rows = given[0].shape[0] - 3 * own_blocks
    return pl.pallas_call(
        functools.partial(halo_features_kernel, block_total, own_blocks),
        out_shape=(
            pltpu.VMEM((len(given) * own_blocks, FEATURES, BLOCK), bf16),
            jax.ShapeDtypeStruct((len(given), list_rows, BLOCK), i32),
        ),
        in_specs=[vmem()] * (len(given) + 1),
        out_specs=(vmem(), vmem()),
        scratch_shapes=[pltpu.VMEM((16, 8, BLOCK), f32), pltpu.VMEM((8, BLOCK), i32)],
        compiler_params=params(8),
        cost_estimate=lasting(1),
        name="halo_features",
    )(sent, *given)


def value_rows(first, second):
    row = lax.broadcasted_iota(i32, (8, BLOCK), 0)
    both = jnp.where((row & 1) == 1, first, second)
    high, middle, low = split(both)
    rows = jnp.where(row < 5, jnp.where(row < 3, high, middle), jnp.where(row < 7, low, 0.0))
    rows = jnp.where(row == 0, 1.0, rows).astype(bf16)
    return jnp.concatenate([rows, rows], axis=1)


def half_kernel(event_ref, mine_ref, near_ref, out_ref):
    half = out_ref.shape[1]
    at = pl.ds(pl.multiple_of((event_ref[0] & 1) * half, half), half)
    out_ref[...] = mine_ref[:, at] + near_ref[:, at]


def half_sum(event, mine, near):
    return pl.pallas_call(
        half_kernel,
        out_shape=jax.ShapeDtypeStruct((2, mine.shape[1] // 2), f32),
        in_specs=[smem(), vmem(), vmem()],
        out_specs=vmem(),
        compiler_params=params(4),
        cost_estimate=lasting(0.1),
        name="half_sum",
    )(event, mine, near)


def add_kernel(first_ref, second_ref, out_ref):
    out_ref[...] = first_ref[...] + second_ref[...]


def added(first, second):
    return pl.pallas_call(
        add_kernel,
        out_shape=jax.ShapeDtypeStruct(first.shape, f32),
        in_specs=[vmem(), vmem()],
        out_specs=vmem(),
        compiler_params=params(4),
        cost_estimate=lasting(0.1),
        name="added",
    )(first, second)


def values_kernel(event_ref, *refs):
    *given, value_ref = refs
    piece_blocks = given[0].shape[1] // BLOCK
    for piece, ref in enumerate(given):
        start = 0 if len(given) == 1 else ((event_ref[0] + piece) & 1) * piece_blocks

        def one_block(b, _):
            at = pl.ds(pl.multiple_of(b * BLOCK, BLOCK), BLOCK)
            value_ref[start + b] = value_rows(ref[0:1, at], ref[1:2, at])
            return 0

        lax.fori_loop(0, piece_blocks, one_block, 0, unroll=16)
    value_ref[value_ref.shape[0] - 1] = jnp.zeros((8, 2 * BLOCK), bf16)


def values_table(event, given, block_total):
    return pl.pallas_call(
        values_kernel,
        out_shape=pltpu.VMEM((block_total + 1, 8, 2 * BLOCK), bf16),
        in_specs=[smem()] + [vmem()] * len(given),
        out_specs=vmem(),
        compiler_params=params(8),
        cost_estimate=lasting(1),
        name="values_table",
    )(event, *given)


def totals_kernel(own_blocks, list_ref, source_ref, target_ref, value_ref, *refs):
    chunks = PAIRS // 2
    *out_refs, sum_ref, weight_ref, exponent_ref = refs
    sets, list_rows = list_ref.shape[0], list_ref.shape[1] - 8
    total_steps = list_ref[0, list_rows, 0]
    for s in range(1, sets):
        total_steps = total_steps + list_ref[s, list_rows, 0]

    def pair(s, k, i):
        at = k * PAIRS + i
        code = list_ref[s, at >> 7, at & (BLOCK - 1)]
        return s * own_blocks + (code >> 10), code & (CODE - 1)

    def following(s, k):
        ends = k + 1 >= list_ref[s, list_rows, 0]
        after = jnp.minimum(jnp.where(ends, s + 1, s), sets - 1)
        return after, jnp.where(ends, 0, k + 1)

    def exponents(s, k, c):
        for h in range(2):
            t, b = pair(s, k, 2 * c + h)
            at = slice(h * BLOCK, (h + 1) * BLOCK)
            exponent_ref[c, :, at] = jnp.dot(
                source_ref[b], target_ref[t], preferred_element_type=f32
            )

    def weights(c):
        weight = jnp.exp2(exponent_ref[c])
        high = weight.astype(bf16)
        weight_ref[c, 0:BLOCK] = high
        weight_ref[c, BLOCK : 2 * BLOCK] = (weight - high.astype(f32)).astype(bf16)

    def sums(s, k, c):
        t0, b0 = pair(s, k, 2 * c)
        t1, b1 = pair(s, k, 2 * c + 1)
        values = jnp.concatenate([value_ref[b0], value_ref[b1]], axis=0)
        both = jnp.dot(values, weight_ref[c], preferred_element_type=f32)
        sum_ref[pl.ds(pl.multiple_of(t0 * 8, 8), 8), :] += both[0:8, 0:BLOCK]
        sum_ref[pl.ds(pl.multiple_of(t1 * 8, 8), 8), :] += both[8:16, BLOCK : 2 * BLOCK]

    sum_ref[...] = jnp.zeros(sum_ref.shape, f32)
    zero = jnp.int32(0)
    for c in range(chunks):
        exponents(zero, zero, c)

    def step(_, at):
        s, k, s_next, k_next = at
        for c in range(chunks):
            weights(c)
            sums(s, k, c)
            exponents(s_next, k_next, c)
        return s_next, k_next, *following(s_next, k_next)

    lax.fori_loop(0, total_steps, step, (zero, zero, *following(zero, zero)))

    for s in range(sets):
        rows = [
            sum_ref[pl.ds(s * own_blocks * 8 + r, own_blocks, stride=8), :] for r in range(7)
        ]
        out_refs[s][0] = rows[0]
        out_refs[s][1] = rows[1] + rows[3] + rows[5]
        out_refs[s][2] = rows[2] + rows[4] + rows[6]


def totals_of(name, lists, sources, targets, values, own_blocks):
    sets = lists.shape[0]
    return pl.pallas_call(
        functools.partial(totals_kernel, own_blocks),
        out_shape=(jax.ShapeDtypeStruct((3, own_blocks, BLOCK), f32),) * sets,
        in_specs=[smem(), vmem(), vmem(), vmem()],
        out_specs=(vmem(),) * sets,
        scratch_shapes=[
            pltpu.VMEM((sets * own_blocks * 8, BLOCK), f32),
            pltpu.VMEM((PAIRS // 2, 2 * BLOCK, 2 * BLOCK), bf16),
            pltpu.VMEM((PAIRS // 2, BLOCK, 2 * BLOCK), f32),
        ],
        compiler_params=params(14),
        cost_estimate=lasting(8),
        name=name,
    )(lists, *held(sources, targets, values))


def local(partials, coords, volume, send_blocks, halo_counts, source_slots, source_counts):
    cut_count = lax.axis_size("cuts")
    event_count = lax.axis_size("event")
    block_total = volume.shape[0] // BLOCK
    own_blocks = source_slots.shape[2]
    grid_step = cut_count // 4
    my_event = lax.axis_index("event")

    strides = [(1, [[0], [1]])]
    if grid_step == 1:
        strides = [(1, [[0, 2], [1, 3]])]
    else:
        strides.append((grid_step, [[2], [3]]))
    event = my_event.reshape(1)
    near_coords, near_volume, own_lists, *parcels = prepare(
        strides, send_blocks.shape[3], event, lax.axis_index("cuts").reshape(1), halo_counts[0],
        source_slots[0, 0].T, source_counts[0], coords, volume.reshape(block_total, BLOCK),
    )
    turns = [(stride, turn) for stride, _ in strides for turn in range(2)]
    arrived = [swapped(p, *turn) for p, turn in zip(parcels, turns)]

    mine = partials[0]
    if event_count == 4:
        part = half_sum(event, mine, crossed(mine, "event", 1))
        part = added(part, crossed(part, "event", 2))
        summed = [part, crossed(part, "event", 1)]
    else:
        summed = [lax.psum(mine, "event")]

    sources, targets = own_features(event, near_coords, near_volume, own_blocks)
    halo_targets, halo_lists = halo_features(
        send_blocks[0, 0], arrived, block_total, own_blocks
    )
    values = values_table(event, summed, block_total)
    halo_totals = totals_of("halo_totals", halo_lists, sources, halo_targets, values, own_blocks)
    returned = [swapped(t, *turn) for t, turn in zip(halo_totals, turns)]
    own_totals = totals_of("own_totals", own_lists, sources, targets, values, own_blocks)
    totals = own_totals[0]
    for part in returned:
        totals = totals + part
    return (totals[1:3] / totals[0]).reshape(2, own_blocks * BLOCK)


def solution(mesh):
    placed = (
        P("event", None, ("runs", "cuts")),
        P(None, ("runs", "cuts")),
        P(("runs", "cuts")),
        P(("runs", "cuts"), "event", None, None),
        P(("runs", "cuts"), "event", None),
        P(("runs", "cuts"), "event", None, None),
        P(("runs", "cuts"), "event", None),
    )
    return jax.shard_map(
        local,
        mesh=mesh,
        in_specs=placed,
        out_specs=P(None, ("runs", "cuts", "event")),
        check_vma=False,
    )
```

```python
import functools
import math

import jax
import jax.numpy as jnp
from jax import lax
from jax.experimental import pallas as pl
from jax.experimental.pallas import tpu as pltpu
from jax.sharding import PartitionSpec as P

BLOCK = 128
FEATURES = 48
STEP_BITS = 4
STEP = 1 << STEP_BITS
FIELD = 10
sigma_km = 50.0
centre_km = 400.0
scale = math.sqrt(math.log2(math.e)) / sigma_km

f32 = jnp.float32
bf16 = jnp.bfloat16
i32 = jnp.int32


def vmem():
    return pl.BlockSpec(memory_space=pltpu.VMEM)


def smem():
    return pl.BlockSpec(memory_space=pltpu.SMEM)


def held(*arrays):
    return [pltpu.with_memory_space_constraint(a, pltpu.VMEM) for a in arrays]


def far(*arrays):
    return [pltpu.with_memory_space_constraint(a, pltpu.HBM) for a in arrays]


def lasting(microseconds):
    flops = int(microseconds * 1.15e9)
    return pl.CostEstimate(flops=flops, bytes_accessed=1000000, transcendentals=0)


def params(mib):
    return pltpu.CompilerParams(vmem_limit_bytes=mib << 20)


def swapped(block, stride, turn):
    devices = lax.axis_size("cuts")
    step = [stride, -stride] if turn == 0 else [-stride, stride]
    route = [(i, (i + step[(i // stride) % 2]) % devices) for i in range(devices)]
    return lax.ppermute(block, "cuts", route)


def crossed(block, axis, bit):
    route = [(i ^ bit, i) for i in range(lax.axis_size(axis))]
    return lax.ppermute(block, axis, route)


def split(values):
    high = values.astype(bf16).astype(f32)
    rest = values - high
    middle = rest.astype(bf16).astype(f32)
    return high, middle, rest - middle


def feature_rows(offsets, fourth, fifth):
    row = lax.broadcasted_iota(i32, (8, BLOCK), 0)
    rows = jnp.where(row == 3, fourth, jnp.where(row == 4, fifth, 0.0))
    return jnp.where(row < 3, offsets, rows)


def place(coords_ref, pad_ref, slot, b):
    at = pl.ds(pl.multiple_of(b * BLOCK, BLOCK), BLOCK)
    pad_ref[slot, 0:3, :] = (coords_ref[:, at] - centre_km) * scale
    offsets = pad_ref[slot]
    return offsets, -0.5 * jnp.sum(offsets * offsets, axis=0, keepdims=True)


def target_features(offsets, norm):
    high, middle, low = split(feature_rows(offsets, 1.0, norm))
    return jnp.concatenate([high, middle, low, high, middle, high], axis=0).astype(bf16)


def own_features_kernel(
    event_ref, coords_ref, volume_ref, source_ref, target_ref, mark_ref, pad_ref, log_ref
):
    block_total = volume_ref.shape[0]
    own_blocks = target_ref.shape[0]
    slots = pad_ref.shape[0]
    pad_ref[...] = jnp.zeros(pad_ref.shape, f32)
    log_ref[...] = jnp.log2(volume_ref[...])

    def some_sources(n, _):
        for slot in range(slots):
            b = n * slots + slot
            offsets, norm = place(coords_ref, pad_ref, slot, b)
            high, middle, low = split(feature_rows(offsets, norm + log_ref[pl.ds(b, 1), :], 1.0))
            rows = jnp.concatenate([high, high, high, middle, middle, low], axis=0)
            source_ref[b] = rows.astype(bf16).T
        return 0

    def some_targets(n, _):
        for slot in range(slots):
            t = n * slots + slot
            block = event_ref[0] * own_blocks + t
            target_ref[t] = target_features(*place(coords_ref, pad_ref, slot, block))
        return 0

    lax.fori_loop(0, block_total // slots, some_sources, 0)
    lax.fori_loop(0, own_blocks // slots, some_targets, 0)
    column = lax.broadcasted_iota(i32, (BLOCK, FEATURES), 1)
    source_ref[block_total] = jnp.where(column == 3, -10000.0, 0.0).astype(bf16)
    mark_ref[...] = jnp.zeros(mark_ref.shape, f32)


def own_features(event, coords, volume, own_blocks):
    block_total = volume.shape[0]
    return pl.pallas_call(
        own_features_kernel,
        out_shape=(
            pltpu.VMEM((block_total + 1, BLOCK, FEATURES), bf16),
            pltpu.VMEM((own_blocks, FEATURES, BLOCK), bf16),
            jax.ShapeDtypeStruct((8, BLOCK), f32),
        ),
        in_specs=[smem(), vmem(), vmem()],
        out_specs=(vmem(),) * 3,
        scratch_shapes=[pltpu.VMEM((16, 8, BLOCK), f32), pltpu.VMEM((block_total, BLOCK), f32)],
        compiler_params=params(8),
        cost_estimate=lasting(4),
        name="own_features",
    )(event, *held(coords, volume))


def coded(target, first, second):
    return (target << (2 * FIELD)) + (second << FIELD) + first


def decoded(code):
    mask = (1 << FIELD) - 1
    return code >> (2 * FIELD), code & mask, (code >> FIELD) & mask


def prepare_kernel(
    strides, capacity, event_ref, cut_ref, halo_given, slot_given, count_given, coords_given,
    volume_given, mine_given, coords_ref, volume_ref, mine_ref, own_ref, *refs,
):
    parcels, rest = refs[: 2 * len(strides)], refs[2 * len(strides) :]
    halo_ref, slot_ref, count_ref, row_ref, list_ref, arrival = rest
    width, own_blocks = slot_ref.shape
    block_total = volume_ref.shape[0]
    sets = len(parcels) + 1
    brought = [
        (halo_given, halo_ref), (slot_given, slot_ref), (count_given, count_ref),
        (coords_given, coords_ref), (volume_given, volume_ref), (mine_given, mine_ref),
    ]
    half = mine_ref.shape[1]
    at = pl.ds(pl.multiple_of((event_ref[0] & 1) * half, half), half)
    brought[5] = (mine_given.at[:, at], mine_ref)
    brought = [
        pltpu.make_async_copy(given, ref, arrival.at[n]) for n, (given, ref) in enumerate(brought)
    ]
    for copy in brought:
        copy.start()
    for copy in brought[:3]:
        copy.wait()
    row_ref[...] = jnp.zeros(row_ref.shape, i32)
    row_ref[0:width, 0:own_blocks] = slot_ref[...]
    row_ref[width : width + 1, 0:own_blocks] = count_ref[...]
    shape = (width, BLOCK)
    slots = row_ref[0:width]
    used = lax.broadcasted_iota(i32, shape, 0) < row_ref[width : width + 1]
    halo = slots - block_total
    lives = [used & (halo < 0)]
    for stride, members in strides:
        both = []
        for directions in members:
            live = jnp.zeros(shape, i32)
            for k in directions:
                near = (halo >= k * capacity) & (halo - k * capacity < halo_ref[0, k])
                live = live + (near & (halo < (k + 1) * capacity)).astype(i32)
            both.append(live)
        odd = (cut_ref[0] // stride) % 2
        for first, second in (both[::-1], both):
            live = first * (1 - odd) + second * odd
            lives.append(used & (live > 0))
    rows = sets * width
    live = jnp.concatenate([l.astype(f32) for l in lives], axis=0).astype(bf16)
    near = lax.broadcasted_iota(i32, (rows, rows), 0)
    across = lax.broadcasted_iota(i32, (rows, rows), 1)
    alike = near // width == across // width
    above = (alike & (across < near)).astype(f32).astype(bf16)
    rank = jnp.dot(above, live, preferred_element_type=f32).astype(i32)
    count = jnp.dot(alike.astype(f32).astype(bf16), live, preferred_element_type=f32)
    twos = ((count.astype(i32) + 1) >> 1).astype(f32).astype(bf16)
    near = lax.broadcasted_iota(i32, (BLOCK, BLOCK), 0)
    across = lax.broadcasted_iota(i32, (BLOCK, BLOCK), 1)
    earlier = (near < across).astype(f32).astype(bf16)
    before = jnp.dot(twos, earlier, preferred_element_type=f32).astype(i32)
    total = jnp.dot(twos, jnp.ones((BLOCK, BLOCK), bf16), preferred_element_type=f32).astype(i32)
    place_of = before + (rank >> 1)
    list_rows = own_blocks * width // (2 * BLOCK)
    high = jnp.full(shape, -1, i32)
    low = jnp.zeros(shape, i32)
    odd = jnp.zeros(shape, i32)
    for s in range(sets):
        part = slice(s * width, (s + 1) * width)
        high = jnp.where(lives[s], (place_of[part] >> 7) + s * list_rows, high)
        low = jnp.where(lives[s], place_of[part] & (BLOCK - 1), low)
        odd = jnp.where(lives[s], rank[part] & 1, odd)
    block = jnp.where(halo < 0, slots, halo) + 1
    even = 1 - odd
    target = lax.broadcasted_iota(i32, shape, 1)
    parts = [target * even, (block >> 3) * even, (block & 7) * even]
    parts = [p.astype(f32) for p in parts + [(block >> 3) * odd, (block & 7) * odd]]
    size = (sets * list_rows + 7) // 8 * 8
    list_row = lax.broadcasted_iota(i32, (size, BLOCK), 0)
    list_lane = lax.broadcasted_iota(i32, (BLOCK, BLOCK), 0)
    codes, places = [], []
    for i in range(width):
        hit = list_row == high[i : i + 1, :]
        codes.append(
            jnp.concatenate([jnp.where(hit, p[i : i + 1, :], 0.0) for p in parts], axis=0)
        )
        places.append((list_lane == low[i : i + 1, :]).astype(f32).astype(bf16))
    codes = jnp.concatenate([c.astype(bf16) for c in codes], axis=1)
    places = jnp.concatenate(places, axis=1)
    found = lax.dot_general(
        codes, places, (((1,), (1,)), ((), ())), preferred_element_type=f32
    ).astype(i32)
    target, *found = [found[n * size : (n + 1) * size] for n in range(5)]
    blocks = [found[0] * 8 + found[1] - 1, found[2] * 8 + found[3] - 1]
    for s in range(sets):
        part = slice(s * list_rows, (s + 1) * list_rows)
        spare = block_total if s == 0 else 4 * capacity
        pair = [jnp.where(b[part] < 0, spare, b[part]) for b in blocks]
        steps = jnp.maximum((total[s * width : s * width + 4] + STEP - 1) >> STEP_BITS, 1)
        if s == 0:
            list_ref[0, 0:list_rows] = coded(target[part], *pair)
            list_ref[0, list_rows:] = steps
        else:
            given = [*pair, target[part], steps]
            for n, values in enumerate(given):
                at = 3 * own_blocks + n * list_rows
                parcels[s - 1][at : at + list_rows] = values.astype(f32)
    sent = pltpu.make_async_copy(list_ref, own_ref, arrival.at[6])
    sent.start()
    for copy in brought[3:]:
        copy.wait()

    def some_coords(t, _):
        at = pl.multiple_of((event_ref[0] * own_blocks + t) * BLOCK, BLOCK)
        given = coords_ref[:, pl.ds(at, BLOCK)]
        for parcel in parcels:
            for r in range(3):
                parcel[pl.ds(r * own_blocks + t, 1), :] = given[r : r + 1]
        return 0

    lax.fori_loop(0, own_blocks, some_coords, 0, unroll=8)
    sent.wait()


def prepare(strides, capacity, event, cut, halo_counts, slots, counts, coords, volume, mine):
    width, own_blocks = slots.shape
    list_rows = own_blocks * width // (2 * BLOCK)
    parcel = jax.ShapeDtypeStruct((3 * own_blocks + 4 * list_rows, BLOCK), f32)
    return pl.pallas_call(
        functools.partial(prepare_kernel, strides, capacity),
        out_shape=(
            pltpu.VMEM(coords.shape, f32),
            pltpu.VMEM(volume.shape, f32),
            pltpu.VMEM((2, mine.shape[1] // 2), f32),
            pltpu.SMEM((1, list_rows + 4, BLOCK), i32),
        )
        + (parcel,) * (2 * len(strides)),
        in_specs=[smem()] * 2 + [pl.BlockSpec(memory_space=pltpu.HBM)] * 6,
        out_specs=(vmem(), vmem(), vmem(), smem()) + (vmem(),) * (2 * len(strides)),
        scratch_shapes=[
            pltpu.SMEM(halo_counts.shape, i32),
            pltpu.VMEM(slots.shape, i32),
            pltpu.VMEM(counts.shape, i32),
            pltpu.VMEM((width + 8, BLOCK), i32),
            pltpu.VMEM((1, list_rows + 4, BLOCK), i32),
            pltpu.SemaphoreType.DMA((7,)),
        ],
        compiler_params=params(8),
        cost_estimate=lasting(2),
        name="prepare",
    )(event, cut, *far(halo_counts, slots, counts, coords, volume, mine))


def halo_features_kernel(block_total, own_blocks, sent_ref, *refs):
    *given, target_ref, smem_ref, list_ref, pad_ref, row_ref, arrival = refs
    slots = pad_ref.shape[0]
    directions, capacity = sent_ref.shape
    pad_ref[...] = jnp.zeros(pad_ref.shape, f32)
    row_ref[...] = jnp.zeros(row_ref.shape, i32)
    row_ref[0:directions, 0:capacity] = sent_ref[...]
    head = 3 * own_blocks
    list_rows = list_ref.shape[1] - 4
    for s, ref in enumerate(given):
        slot = ref[head : head + 2 * list_rows].astype(i32)
        block = jnp.full(slot.shape, block_total, i32)
        for k in range(directions):
            here = (slot >= k * capacity) & (slot < (k + 1) * capacity)
            row = jnp.broadcast_to(row_ref[k : k + 1, :], slot.shape)
            at = jnp.where(here, slot - k * capacity, 0)
            block = jnp.where(here, jnp.take_along_axis(row, at, axis=1), block)
        rest = ref[head + 2 * list_rows :].astype(i32)
        list_ref[s, 0:list_rows] = coded(rest[0:list_rows], block[0:list_rows], block[list_rows:])
        list_ref[s, list_rows:] = rest[list_rows:]
    sent = pltpu.make_async_copy(list_ref, smem_ref, arrival)
    sent.start()
    for s, ref in enumerate(given):

        def some_targets(n, _):
            for q in range(slots):
                t = n * slots + q
                for r in range(3):
                    row = ref[pl.ds(r * own_blocks + t, 1), :]
                    pad_ref[q, r : r + 1, :] = (row - centre_km) * scale
                offsets = pad_ref[q]
                norm = -0.5 * jnp.sum(offsets * offsets, axis=0, keepdims=True)
                target_ref[s * own_blocks + t] = target_features(offsets, norm)
            return 0

        lax.fori_loop(0, own_blocks // slots, some_targets, 0)
    sent.wait()


def halo_features(sent, given, block_total, own_blocks):
    list_rows = (given[0].shape[0] - 3 * own_blocks) // 4
    lists = (len(given), list_rows + 4, BLOCK)
    return pl.pallas_call(
        functools.partial(halo_features_kernel, block_total, own_blocks),
        out_shape=(
            pltpu.VMEM((len(given) * own_blocks, FEATURES, BLOCK), bf16),
            pltpu.SMEM(lists, i32),
        ),
        in_specs=[vmem()] * (len(given) + 1),
        out_specs=(vmem(), smem()),
        scratch_shapes=[
            pltpu.VMEM(lists, i32),
            pltpu.VMEM((16, 8, BLOCK), f32),
            pltpu.VMEM((8, BLOCK), i32),
            pltpu.SemaphoreType.DMA,
        ],
        compiler_params=params(8),
        cost_estimate=lasting(1),
        name="halo_features",
    )(sent, *given)


def value_rows(first, second):
    row = lax.broadcasted_iota(i32, (8, BLOCK), 0)
    both = jnp.where((row & 1) == 1, first, second)
    high, middle, low = split(both)
    rows = jnp.where(row < 5, jnp.where(row < 3, high, middle), jnp.where(row < 7, low, 0.0))
    rows = jnp.where(row == 0, 1.0, rows).astype(bf16)
    return jnp.concatenate([rows, rows], axis=1)


def half_kernel(event_ref, mine_ref, near_ref, out_ref):
    half = out_ref.shape[1]
    at = pl.ds(pl.multiple_of((event_ref[0] & 1) * half, half), half)
    out_ref[...] = mine_ref[...] + near_ref[:, at]


def half_sum(event, mine, near):
    return pl.pallas_call(
        half_kernel,
        out_shape=jax.ShapeDtypeStruct(mine.shape, f32),
        in_specs=[smem(), vmem(), vmem()],
        out_specs=vmem(),
        compiler_params=params(4),
        cost_estimate=lasting(0.1),
        name="half_sum",
    )(event, *held(mine), near)


def add_kernel(first_ref, second_ref, mark_ref, out_ref):
    out_ref[...] = first_ref[...] + second_ref[...]


def added(first, second, mark):
    return pl.pallas_call(
        add_kernel,
        out_shape=jax.ShapeDtypeStruct(first.shape, f32),
        in_specs=[vmem()] * 3,
        out_specs=vmem(),
        compiler_params=params(4),
        cost_estimate=lasting(0.1),
        name="added",
    )(first, second, mark)


def values_kernel(event_ref, *refs):
    *given, value_ref = refs
    piece_blocks = given[0].shape[1] // BLOCK
    for piece, ref in enumerate(given):
        start = 0 if len(given) == 1 else ((event_ref[0] + piece) & 1) * piece_blocks

        def one_block(b, _):
            at = pl.ds(pl.multiple_of(b * BLOCK, BLOCK), BLOCK)
            value_ref[start + b] = value_rows(ref[0:1, at], ref[1:2, at])
            return 0

        lax.fori_loop(0, piece_blocks, one_block, 0, unroll=16)
    value_ref[value_ref.shape[0] - 1] = jnp.zeros((8, 2 * BLOCK), bf16)


def values_table(event, given, block_total):
    return pl.pallas_call(
        values_kernel,
        out_shape=pltpu.VMEM((block_total + 1, 8, 2 * BLOCK), bf16),
        in_specs=[smem()] + [vmem()] * len(given),
        out_specs=vmem(),
        compiler_params=params(8),
        cost_estimate=lasting(1),
        name="values_table",
    )(event, *given)


def totals_kernel(own_blocks, list_ref, source_ref, target_ref, value_ref, *refs):
    *out_refs, sum_ref, weight_ref, exponent_ref = refs
    sets, list_rows = list_ref.shape[0], list_ref.shape[1] - 4
    total_steps = list_ref[0, list_rows, 0]
    for s in range(1, sets):
        total_steps = total_steps + list_ref[s, list_rows, 0]

    def chunk(s, k, c):
        at = k * STEP + c
        t, first, second = decoded(list_ref[s, at >> 7, at & (BLOCK - 1)])
        return s * own_blocks + t, first, second

    def following(s, k):
        ends = k + 1 >= list_ref[s, list_rows, 0]
        after = jnp.minimum(jnp.where(ends, s + 1, s), sets - 1)
        return after, jnp.where(ends, 0, k + 1)

    def exponents(s, k, c):
        t, first, second = chunk(s, k, c)
        both = jnp.concatenate([source_ref[first], source_ref[second]], axis=0)
        exponent = jnp.dot(both, target_ref[t], preferred_element_type=f32)
        exponent_ref[c, :, 0:BLOCK] = exponent[0:BLOCK]
        exponent_ref[c, :, BLOCK:] = exponent[BLOCK:]

    def weights(c):
        weight = jnp.exp2(exponent_ref[c])
        high = weight.astype(bf16)
        weight_ref[c, 0:BLOCK] = high
        weight_ref[c, BLOCK : 2 * BLOCK] = (weight - high.astype(f32)).astype(bf16)

    def sums(s, k, c):
        t, first, second = chunk(s, k, c)
        values = jnp.concatenate([value_ref[first], value_ref[second]], axis=0)
        both = jnp.dot(values, weight_ref[c], preferred_element_type=f32)
        at = pl.ds(pl.multiple_of(t * 8, 8), 8)
        sum_ref[at, :] += both[0:8, 0:BLOCK] + both[8:16, BLOCK : 2 * BLOCK]

    sum_ref[...] = jnp.zeros(sum_ref.shape, f32)
    zero = jnp.int32(0)
    for c in range(STEP):
        exponents(zero, zero, c)

    def step(_, at):
        s, k, s_next, k_next = at
        for c in range(STEP):
            weights(c)
            sums(s, k, c)
            exponents(s_next, k_next, c)
        return s_next, k_next, *following(s_next, k_next)

    lax.fori_loop(0, total_steps, step, (zero, zero, *following(zero, zero)))

    for s in range(sets):
        rows = [
            sum_ref[pl.ds(s * own_blocks * 8 + r, own_blocks, stride=8), :] for r in range(7)
        ]
        out_refs[s][0] = rows[0]
        out_refs[s][1] = rows[1] + rows[3] + rows[5]
        out_refs[s][2] = rows[2] + rows[4] + rows[6]


def totals_of(name, lists, sources, targets, values, own_blocks):
    sets = lists.shape[0]
    return pl.pallas_call(
        functools.partial(totals_kernel, own_blocks),
        out_shape=(jax.ShapeDtypeStruct((3, own_blocks, BLOCK), f32),) * sets,
        in_specs=[smem(), vmem(), vmem(), vmem()],
        out_specs=(vmem(),) * sets,
        scratch_shapes=[
            pltpu.VMEM((sets * own_blocks * 8, BLOCK), f32),
            pltpu.VMEM((STEP, 2 * BLOCK, 2 * BLOCK), bf16),
            pltpu.VMEM((STEP, BLOCK, 2 * BLOCK), f32),
        ],
        compiler_params=params(14),
        cost_estimate=lasting(8),
        name=name,
    )(pltpu.with_memory_space_constraint(lists, pltpu.SMEM), *held(sources, targets, values))


def local(partials, coords, volume, send_blocks, halo_counts, source_slots, source_counts):
    cut_count = lax.axis_size("cuts")
    event_count = lax.axis_size("event")
    block_total = volume.shape[0] // BLOCK
    own_blocks = source_slots.shape[2]
    grid_step = cut_count // 4
    my_event = lax.axis_index("event")

    strides = [(1, [[0], [1]])]
    if grid_step == 1:
        strides = [(1, [[0, 2], [1, 3]])]
    else:
        strides.append((grid_step, [[2], [3]]))
    event = my_event.reshape(1)
    mine = partials[0]
    near_coords, near_volume, near_mine, own_lists, *parcels = prepare(
        strides, send_blocks.shape[3], event, lax.axis_index("cuts").reshape(1), halo_counts[0],
        source_slots[0, 0].T, source_counts[0], coords, volume.reshape(block_total, BLOCK),
        mine,
    )
    turns = [(stride, turn) for stride, _ in strides for turn in range(2)]
    arrived = [swapped(p, *turn) for p, turn in zip(parcels, turns)]

    sources, targets, mark = own_features(event, near_coords, near_volume, own_blocks)
    if event_count == 4:
        part = half_sum(event, near_mine, crossed(mine, "event", 1))
        part = added(part, crossed(part, "event", 2), mark)
        summed = [part, crossed(part, "event", 1)]
    else:
        summed = [lax.psum(mine, "event")]

    halo_targets, halo_lists = halo_features(
        send_blocks[0, 0], arrived, block_total, own_blocks
    )
    values = values_table(event, summed, block_total)
    halo_totals = totals_of("halo_totals", halo_lists, sources, halo_targets, values, own_blocks)
    returned = [swapped(t, *turn) for t, turn in zip(halo_totals, turns)]
    own_totals = totals_of("own_totals", own_lists, sources, targets, values, own_blocks)
    totals = own_totals[0]
    for part in returned:
        totals = totals + part
    return (totals[1:3] / totals[0]).reshape(2, own_blocks * BLOCK)


def solution(mesh):
    placed = (
        P("event", None, ("runs", "cuts")),
        P(None, ("runs", "cuts")),
        P(("runs", "cuts")),
        P(("runs", "cuts"), "event", None, None),
        P(("runs", "cuts"), "event", None),
        P(("runs", "cuts"), "event", None, None),
        P(("runs", "cuts"), "event", None),
    )
    return jax.shard_map(
        local,
        mesh=mesh,
        in_specs=placed,
        out_specs=P(None, ("runs", "cuts", "event")),
        check_vma=False,
    )
```

```python
import functools
import math

import jax
import jax.numpy as jnp
from jax import lax
from jax.experimental import pallas as pl
from jax.experimental.pallas import tpu as pltpu
from jax.sharding import PartitionSpec as P

BLOCK = 128
FEATURES = 48
STEP_BITS = 5
STEP = 1 << STEP_BITS
QUOTA = 6
FIELD = 10
sigma_km = 50.0
centre_km = 400.0
scale = math.sqrt(math.log2(math.e)) / sigma_km

f32 = jnp.float32
bf16 = jnp.bfloat16
i32 = jnp.int32


def vmem():
    return pl.BlockSpec(memory_space=pltpu.VMEM)


def smem():
    return pl.BlockSpec(memory_space=pltpu.SMEM)


def held(*arrays):
    return [pltpu.with_memory_space_constraint(a, pltpu.VMEM) for a in arrays]


def far(*arrays):
    return [pltpu.with_memory_space_constraint(a, pltpu.HBM) for a in arrays]


def lasting(microseconds):
    flops = int(microseconds * 1.15e9)
    return pl.CostEstimate(flops=flops, bytes_accessed=1000000, transcendentals=0)


def params(mib):
    return pltpu.CompilerParams(vmem_limit_bytes=mib << 20)


def swapped(block, stride, turn):
    devices = lax.axis_size("cuts")
    step = [stride, -stride] if turn == 0 else [-stride, stride]
    route = [(i, (i + step[(i // stride) % 2]) % devices) for i in range(devices)]
    return lax.ppermute(block, "cuts", route)


def crossed(block, axis, bit):
    route = [(i ^ bit, i) for i in range(lax.axis_size(axis))]
    return lax.ppermute(block, axis, route)


def split(values):
    high = values.astype(bf16).astype(f32)
    rest = values - high
    middle = rest.astype(bf16).astype(f32)
    return high, middle, rest - middle


def feature_rows(offsets, fourth, fifth):
    row = lax.broadcasted_iota(i32, (8, BLOCK), 0)
    rows = jnp.where(row == 3, fourth, jnp.where(row == 4, fifth, 0.0))
    return jnp.where(row < 3, offsets, rows)


def place(coords_ref, pad_ref, slot, b):
    at = pl.ds(pl.multiple_of(b * BLOCK, BLOCK), BLOCK)
    pad_ref[slot, 0:3, :] = (coords_ref[:, at] - centre_km) * scale
    offsets = pad_ref[slot]
    return offsets, -0.5 * jnp.sum(offsets * offsets, axis=0, keepdims=True)


def target_features(offsets, norm):
    high, middle, low = split(feature_rows(offsets, 1.0, norm))
    return jnp.concatenate([high, middle, low, high, middle, high], axis=0).astype(bf16)


def own_features_kernel(
    event_ref, coords_ref, volume_ref, source_ref, target_ref, mark_ref, pad_ref, log_ref
):
    block_total = volume_ref.shape[0]
    own_blocks = target_ref.shape[0]
    slots = pad_ref.shape[0]
    pad_ref[...] = jnp.zeros(pad_ref.shape, f32)
    log_ref[...] = jnp.log2(volume_ref[...])

    def some_sources(n, _):
        for slot in range(slots):
            b = n * slots + slot
            offsets, norm = place(coords_ref, pad_ref, slot, b)
            high, middle, low = split(feature_rows(offsets, norm + log_ref[pl.ds(b, 1), :], 1.0))
            rows = jnp.concatenate([high, high, high, middle, middle, low], axis=0)
            source_ref[b] = rows.astype(bf16).T
        return 0

    def some_targets(n, _):
        for slot in range(slots):
            t = n * slots + slot
            block = event_ref[0] * own_blocks + t
            target_ref[t] = target_features(*place(coords_ref, pad_ref, slot, block))
        return 0

    lax.fori_loop(0, block_total // slots, some_sources, 0)
    lax.fori_loop(0, own_blocks // slots, some_targets, 0)
    column = lax.broadcasted_iota(i32, (BLOCK, FEATURES), 1)
    source_ref[block_total] = jnp.where(column == 3, -10000.0, 0.0).astype(bf16)
    mark_ref[...] = jnp.zeros(mark_ref.shape, f32)


def own_features(event, coords, volume, own_blocks):
    block_total = volume.shape[0]
    return pl.pallas_call(
        own_features_kernel,
        out_shape=(
            pltpu.VMEM((block_total + 1, BLOCK, FEATURES), bf16),
            pltpu.VMEM((own_blocks, FEATURES, BLOCK), bf16),
            jax.ShapeDtypeStruct((8, BLOCK), f32),
        ),
        in_specs=[smem(), vmem(), vmem()],
        out_specs=(vmem(),) * 3,
        scratch_shapes=[
            pltpu.VMEM((16, 8, BLOCK), f32),
            pltpu.VMEM((block_total, BLOCK), f32),
        ],
        compiler_params=params(8),
        cost_estimate=lasting(4),
        name="own_features",
    )(event, *held(coords, volume))


def coded(target, first, second):
    return (target << (2 * FIELD)) + (second << FIELD) + first


def finished_list(ref, codes, spare, count):
    list_rows = codes.shape[0]
    ref[0:list_rows] = codes
    ref[list_rows : list_rows + 1] = jnp.full((1, BLOCK), coded(0, spare, spare), i32)
    ref[list_rows + 1 :] = count[0:3]


def decoded(code):
    mask = (1 << FIELD) - 1
    return code >> (2 * FIELD), code & mask, (code >> FIELD) & mask


def prepare_kernel(
    strides, capacity, event_ref, cut_ref, halo_given, slot_given, count_given, coords_given,
    volume_given, mine_given, coords_ref, volume_ref, mine_ref, own_ref, *refs,
):
    parcels, rest = refs[: 2 * len(strides)], refs[2 * len(strides) :]
    halo_ref, slot_ref, count_ref, row_ref, arrival = rest
    width, own_blocks = slot_ref.shape
    block_total = volume_ref.shape[0]
    sets = len(parcels) + 1
    brought = [
        (halo_given, halo_ref), (slot_given, slot_ref), (count_given, count_ref),
        (coords_given, coords_ref), (volume_given, volume_ref), (mine_given, mine_ref),
    ]
    half = mine_ref.shape[1]
    at = pl.ds(pl.multiple_of((event_ref[0] & 1) * half, half), half)
    brought[5] = (mine_given.at[:, at], mine_ref)
    brought = [
        pltpu.make_async_copy(given, ref, arrival.at[n]) for n, (given, ref) in enumerate(brought)
    ]
    for copy in brought:
        copy.start()
    for copy in brought[:3]:
        copy.wait()
    row_ref[...] = jnp.zeros(row_ref.shape, i32)
    row_ref[0:width, 0:own_blocks] = slot_ref[...]
    row_ref[width : width + 1, 0:own_blocks] = count_ref[...]
    shape = (width, BLOCK)
    slots = row_ref[0:width]
    used = lax.broadcasted_iota(i32, shape, 0) < row_ref[width : width + 1]
    halo = slots - block_total
    lives = [used & (halo < 0)]
    for stride, members in strides:
        both = []
        for directions in members:
            live = jnp.zeros(shape, i32)
            for k in directions:
                near = (halo >= k * capacity) & (halo - k * capacity < halo_ref[0, k])
                live = live + (near & (halo < (k + 1) * capacity)).astype(i32)
            both.append(live)
        odd = (cut_ref[0] // stride) % 2
        for first, second in (both, both[::-1]):
            live = first * (1 - odd) + second * odd
            lives.append(used & (live > 0))
    rows = sets * width
    live = jnp.concatenate([l.astype(f32) for l in lives], axis=0).astype(bf16)
    near = lax.broadcasted_iota(i32, (rows, rows), 0)
    across = lax.broadcasted_iota(i32, (rows, rows), 1)
    alike = near // width == across // width
    above = (alike & (across < near)).astype(f32).astype(bf16)
    rank = jnp.dot(above, live, preferred_element_type=f32).astype(i32)
    count = jnp.dot(alike.astype(f32).astype(bf16), live, preferred_element_type=f32)
    twos = ((count.astype(i32) + 1) >> 1).astype(f32).astype(bf16)
    near = lax.broadcasted_iota(i32, (BLOCK, BLOCK), 0)
    across = lax.broadcasted_iota(i32, (BLOCK, BLOCK), 1)
    earlier = (near < across).astype(f32).astype(bf16)
    before = jnp.dot(twos, earlier, preferred_element_type=f32).astype(i32)
    total = jnp.dot(twos, jnp.ones((BLOCK, BLOCK), bf16), preferred_element_type=f32).astype(i32)
    place_of = before + (rank >> 1)
    list_rows = own_blocks * width // (2 * BLOCK)
    high = jnp.full(shape, -1, i32)
    low = jnp.zeros(shape, i32)
    odd = jnp.zeros(shape, i32)
    for s in range(sets):
        part = slice(s * width, (s + 1) * width)
        high = jnp.where(lives[s], (place_of[part] >> 7) + s * list_rows, high)
        low = jnp.where(lives[s], place_of[part] & (BLOCK - 1), low)
        odd = jnp.where(lives[s], rank[part] & 1, odd)
    block = jnp.where(halo < 0, slots, halo) + 1
    even = 1 - odd
    target = lax.broadcasted_iota(i32, shape, 1)
    parts = [target * even, (block >> 3) * even, (block & 7) * even]
    parts = [p.astype(f32) for p in parts + [(block >> 3) * odd, (block & 7) * odd]]
    size = (sets * list_rows + 7) // 8 * 8
    list_row = lax.broadcasted_iota(i32, (size, BLOCK), 0)
    list_lane = lax.broadcasted_iota(i32, (BLOCK, BLOCK), 0)
    codes, places = [], []
    for i in range(width):
        hit = list_row == high[i : i + 1, :]
        codes.append(
            jnp.concatenate([jnp.where(hit, p[i : i + 1, :], 0.0) for p in parts], axis=0)
        )
        places.append((list_lane == low[i : i + 1, :]).astype(f32).astype(bf16))
    codes = jnp.concatenate([c.astype(bf16) for c in codes], axis=1)
    places = jnp.concatenate(places, axis=1)
    found = lax.dot_general(
        codes, places, (((1,), (1,)), ((), ())), preferred_element_type=f32
    ).astype(i32)
    target, *found = [found[n * size : (n + 1) * size] for n in range(5)]
    blocks = [found[0] * 8 + found[1] - 1, found[2] * 8 + found[3] - 1]
    for s in range(sets):
        part = slice(s * list_rows, (s + 1) * list_rows)
        spare = block_total if s == 0 else 4 * capacity
        pair = [jnp.where(b[part] < 0, spare, b[part]) for b in blocks]
        count = total[s * width : s * width + list_rows]
        if s == 0:
            finished_list(own_ref, coded(target[part], *pair), spare, count)
        else:
            given = [*pair, target[part], count]
            for n, values in enumerate(given):
                at = 3 * own_blocks + n * list_rows
                parcels[s - 1][at : at + list_rows] = values.astype(f32)
    for copy in brought[3:]:
        copy.wait()

    def some_coords(t, _):
        at = pl.multiple_of((event_ref[0] * own_blocks + t) * BLOCK, BLOCK)
        given = coords_ref[:, pl.ds(at, BLOCK)]
        for parcel in parcels:
            for r in range(3):
                parcel[pl.ds(r * own_blocks + t, 1), :] = given[r : r + 1]
        return 0

    lax.fori_loop(0, own_blocks, some_coords, 0, unroll=8)


def prepare(strides, capacity, event, cut, halo_counts, slots, counts, coords, volume, mine):
    width, own_blocks = slots.shape
    list_rows = own_blocks * width // (2 * BLOCK)
    parcel = jax.ShapeDtypeStruct((3 * own_blocks + 4 * list_rows, BLOCK), f32)
    return pl.pallas_call(
        functools.partial(prepare_kernel, strides, capacity),
        out_shape=(
            pltpu.VMEM(coords.shape, f32),
            pltpu.VMEM(volume.shape, f32),
            pltpu.VMEM((2, mine.shape[1] // 2), f32),
            pltpu.VMEM((list_rows + 4, BLOCK), i32),
        )
        + (parcel,) * (2 * len(strides)),
        in_specs=[smem()] * 2 + [pl.BlockSpec(memory_space=pltpu.HBM)] * 6,
        out_specs=(vmem(),) * 4 + (vmem(),) * (2 * len(strides)),
        scratch_shapes=[
            pltpu.SMEM(halo_counts.shape, i32),
            pltpu.VMEM(slots.shape, i32),
            pltpu.VMEM(counts.shape, i32),
            pltpu.VMEM((width + 8, BLOCK), i32),
            pltpu.SemaphoreType.DMA((6,)),
        ],
        compiler_params=params(8),
        cost_estimate=lasting(2),
        name="prepare",
    )(event, cut, *far(halo_counts, slots, counts, coords, volume, mine))


def halo_features_kernel(block_total, own_blocks, own_ref, near_ref, sent_ref, *refs):
    *given, target_ref, smem_ref, list_ref, pad_ref, row_ref, arrival = refs
    slots = pad_ref.shape[0]
    directions, capacity = sent_ref.shape
    pad_ref[...] = jnp.zeros(pad_ref.shape, f32)
    row_ref[...] = jnp.zeros(row_ref.shape, i32)
    row_ref[0:directions, 0:capacity] = sent_ref[...]
    head = 3 * own_blocks
    list_rows = list_ref.shape[1] - 4
    for s, ref in enumerate(given):
        slot = ref[head : head + 2 * list_rows].astype(i32)
        block = jnp.full(slot.shape, block_total, i32)
        for k in range(directions):
            here = (slot >= k * capacity) & (slot < (k + 1) * capacity)
            row = jnp.broadcast_to(row_ref[k : k + 1, :], slot.shape)
            at = jnp.where(here, slot - k * capacity, 0)
            block = jnp.where(here, jnp.take_along_axis(row, at, axis=1), block)
        rest = ref[head + 2 * list_rows :].astype(i32)
        codes = coded(rest[0:list_rows], block[0:list_rows], block[list_rows:])
        finished_list(list_ref.at[s], codes, block_total, rest[list_rows:])
    list_ref[len(given)] = own_ref[...]
    sent = pltpu.make_async_copy(list_ref, smem_ref, arrival)
    sent.start()
    target_ref[len(given) * own_blocks :] = near_ref[...]
    for s, ref in enumerate(given):

        def some_targets(n, _):
            for q in range(slots):
                t = n * slots + q
                for r in range(3):
                    row = ref[pl.ds(r * own_blocks + t, 1), :]
                    pad_ref[q, r : r + 1, :] = (row - centre_km) * scale
                offsets = pad_ref[q]
                norm = -0.5 * jnp.sum(offsets * offsets, axis=0, keepdims=True)
                target_ref[s * own_blocks + t] = target_features(offsets, norm)
            return 0

        lax.fori_loop(0, own_blocks // slots, some_targets, 0)
    sent.wait()


def halo_features(own_list, targets, sent, given, block_total):
    own_blocks = targets.shape[0]
    list_rows = (given[0].shape[0] - 3 * own_blocks) // 4
    lists = (len(given) + 1, list_rows + 4, BLOCK)
    return pl.pallas_call(
        functools.partial(halo_features_kernel, block_total, own_blocks),
        out_shape=(
            pltpu.VMEM(((len(given) + 1) * own_blocks, FEATURES, BLOCK), bf16),
            pltpu.SMEM(lists, i32),
        ),
        in_specs=[vmem()] * (len(given) + 3),
        out_specs=(vmem(), smem()),
        scratch_shapes=[
            pltpu.VMEM(lists, i32),
            pltpu.VMEM((16, 8, BLOCK), f32),
            pltpu.VMEM((8, BLOCK), i32),
            pltpu.SemaphoreType.DMA,
        ],
        compiler_params=params(8),
        cost_estimate=lasting(1),
        name="halo_features",
    )(*held(own_list, targets), sent, *given)


def value_rows(first, second):
    row = lax.broadcasted_iota(i32, (8, BLOCK), 0)
    both = jnp.where((row & 1) == 1, first, second)
    high, middle, low = split(both)
    rows = jnp.where(row < 5, jnp.where(row < 3, high, middle), jnp.where(row < 7, low, 0.0))
    rows = jnp.where(row == 0, 1.0, rows).astype(bf16)
    return jnp.concatenate([rows, rows], axis=1)


def half_kernel(event_ref, mine_ref, near_ref, *refs):
    parcels, (out_ref, *sent) = refs[: len(refs) // 2], refs[len(refs) // 2 :]
    half = out_ref.shape[1]
    at = pl.ds(pl.multiple_of((event_ref[0] & 1) * half, half), half)
    out_ref[...] = mine_ref[...] + near_ref[:, at]
    for given, to in zip(parcels, sent):
        to[...] = given[...]


def half_sum(event, mine, near, parcels):
    return pl.pallas_call(
        half_kernel,
        out_shape=[jax.ShapeDtypeStruct(a.shape, f32) for a in (mine, *parcels)],
        in_specs=[smem()] + [vmem()] * (len(parcels) + 2),
        out_specs=[vmem()] * (len(parcels) + 1),
        compiler_params=params(4),
        cost_estimate=lasting(0.1),
        name="half_sum",
    )(event, *held(mine), near, *parcels)


def add_kernel(first_ref, second_ref, mark_ref, out_ref):
    out_ref[...] = first_ref[...] + second_ref[...]


def added(first, second, mark):
    return pl.pallas_call(
        add_kernel,
        out_shape=jax.ShapeDtypeStruct(first.shape, f32),
        in_specs=[vmem()] * 3,
        out_specs=vmem(),
        compiler_params=params(4),
        cost_estimate=lasting(0.1),
        name="added",
    )(first, second, mark)


def schedule(list_ref):
    sets, list_rows = list_ref.shape[0], list_ref.shape[1] - 4
    ends = []
    for s in range(sets):
        ends.append(list_ref[s, list_rows + 1, 0] + (ends[-1] if ends else 0))
    halo_steps, all_steps = [(e + STEP - 1) >> STEP_BITS for e in ends[-2:]]
    return ends, jnp.maximum(halo_steps, jnp.minimum(QUOTA, all_steps)), all_steps


class Totals:
    def __init__(self, ends, own_blocks, first_set, refs):
        self.ends, self.own_blocks, self.first_set = ends, own_blocks, first_set
        self.lists, self.sources, self.targets, self.values = refs[:4]
        self.exponent_ref, self.weight_ref, self.sum_ref = refs[4:]

    def chunk(self, i):
        s, base = 0, 0
        for end in self.ends[:-1]:
            past = i >= end
            s = s + past.astype(i32)
            base = jnp.where(past, end, base)
        at = i - base
        t, first, second = decoded(self.lists[s, at >> 7, at & (BLOCK - 1)])
        return s * self.own_blocks + t, first, second

    def exponents(self, k, c):
        t, first, second = self.chunk(k * STEP + c)
        both = jnp.concatenate([self.sources[first], self.sources[second]], axis=0)
        exponent = jnp.dot(both, self.targets[t], preferred_element_type=f32)
        self.exponent_ref[c, :, 0:BLOCK] = exponent[0:BLOCK]
        self.exponent_ref[c, :, BLOCK:] = exponent[BLOCK:]

    def weights(self, c):
        weight = jnp.exp2(self.exponent_ref[c])
        high = weight.astype(bf16)
        self.weight_ref[c, 0:BLOCK] = high
        self.weight_ref[c, BLOCK : 2 * BLOCK] = (weight - high.astype(f32)).astype(bf16)

    def sums(self, k, c):
        t, first, second = self.chunk(k * STEP + c)
        values = jnp.concatenate([self.values[first], self.values[second]], axis=0)
        both = jnp.dot(values, self.weight_ref[c], preferred_element_type=f32)
        at = pl.ds(pl.multiple_of((t - self.first_set * self.own_blocks) * 8, 8), 8)
        self.sum_ref[at, :] += both[0:8, 0:BLOCK] + both[8:16, BLOCK : 2 * BLOCK]

    def steps(self, begin, end):
        def step(k, _):
            for c in range(STEP):
                self.weights(c)
                self.sums(k, c)
                self.exponents(k + 1, c)
            return 0

        lax.fori_loop(begin, end, step, 0)

    def finish(self, s, out_ref):
        rows = [
            self.sum_ref[pl.ds(s * self.own_blocks * 8 + r, self.own_blocks, stride=8), :]
            for r in range(7)
        ]
        out_ref[0] = rows[0]
        out_ref[1] = rows[1] + rows[3] + rows[5]
        out_ref[2] = rows[2] + rows[4] + rows[6]


def first_totals_kernel(own_blocks, list_ref, source_ref, target_ref, *refs):
    *refs, sum_ref, weight_ref = refs
    sets = list_ref.shape[0]
    own_sum_ref, value_ref, exponent_ref = refs[-3:]
    out_refs = refs[-3 - (sets - 1) : -3]
    summed = refs[: -3 - (sets - 1)]
    ends, first_steps, _ = schedule(list_ref)
    given = [list_ref, source_ref, target_ref, value_ref, exponent_ref, weight_ref, sum_ref]
    totals = Totals(ends, own_blocks, 0, given)
    sum_ref[...] = jnp.zeros(sum_ref.shape, f32)
    block_total = value_ref.shape[0] - 1
    rounds = 1

    def begin(n, _):
        for c in range(STEP // rounds):
            totals.exponents(0, n * (STEP // rounds) + c)
        for c in range(block_total // rounds):
            b = n * (block_total // rounds) + c
            at = pl.ds(pl.multiple_of(b * BLOCK, BLOCK), BLOCK)
            both = sum(ref[:, at] for ref in summed)
            value_ref[b] = value_rows(both[0:1], both[1:2])
        return 0

    if len(summed) == 1:
        lax.fori_loop(0, rounds, begin, 0)
    else:
        begin_from_halves(totals, summed, value_ref, rounds)
    value_ref[block_total] = jnp.zeros((8, 2 * BLOCK), bf16)
    totals.steps(0, first_steps)
    for s in range(sets - 1):
        totals.finish(s, out_refs[s])
    own_sum_ref[...] = sum_ref[(sets - 1) * own_blocks * 8 :, :]


def begin_from_halves(totals, summed, value_ref, rounds):
    event_ref, *halves = summed
    half_blocks = (value_ref.shape[0] - 1) // 2
    core = event_ref[0] & 1

    def begin(n, _):
        for c in range(STEP // rounds):
            totals.exponents(0, n * (STEP // rounds) + c)
        for piece, ref in enumerate(halves):
            for c in range(half_blocks // rounds):
                b = n * (half_blocks // rounds) + c
                at = pl.ds(pl.multiple_of(b * BLOCK, BLOCK), BLOCK)
                where = (core ^ piece) * half_blocks + b
                totals.values[where] = value_rows(ref[0:1, at], ref[1:2, at])
        return 0

    lax.fori_loop(0, rounds, begin, 0)


def first_totals(lists, sources, targets, summed, block_total):
    sets = lists.shape[0]
    own_blocks = targets.shape[0] // sets
    specs = [smem()] * (len(summed) - 2) + [vmem()] * min(len(summed), 2)
    return pl.pallas_call(
        functools.partial(first_totals_kernel, own_blocks),
        out_shape=[jax.ShapeDtypeStruct((3, own_blocks, BLOCK), f32)] * (sets - 1)
        + [
            pltpu.VMEM((own_blocks * 8, BLOCK), f32),
            pltpu.VMEM((block_total + 1, 8, 2 * BLOCK), bf16),
            pltpu.VMEM((STEP, BLOCK, 2 * BLOCK), f32),
        ],
        in_specs=[smem(), vmem(), vmem()] + specs,
        out_specs=[vmem()] * (sets + 2),
        scratch_shapes=[
            pltpu.VMEM((sets * own_blocks * 8, BLOCK), f32),
            pltpu.VMEM((STEP, 2 * BLOCK, 2 * BLOCK), bf16),
        ],
        compiler_params=params(14),
        cost_estimate=lasting(8),
        name="first_totals",
    )(pltpu.with_memory_space_constraint(lists, pltpu.SMEM), *held(sources, targets), *summed)


def last_totals_kernel(
    own_blocks, list_ref, source_ref, target_ref, value_ref, own_sum_ref, _, out_ref,
    exponent_ref, sum_ref, weight_ref,
):
    ends, first_steps, all_steps = schedule(list_ref)
    given = [list_ref, source_ref, target_ref, value_ref, exponent_ref, weight_ref, sum_ref]
    totals = Totals(ends, own_blocks, list_ref.shape[0] - 1, given)
    sum_ref[...] = own_sum_ref[...]
    totals.steps(first_steps, all_steps)
    totals.finish(0, out_ref)


def last_totals(lists, sources, targets, values, own_sum, exponent):
    own_blocks = targets.shape[0] // lists.shape[0]
    lists = pltpu.with_memory_space_constraint(lists, pltpu.SMEM)
    total, _ = pl.pallas_call(
        functools.partial(last_totals_kernel, own_blocks),
        out_shape=[
            jax.ShapeDtypeStruct((3, own_blocks, BLOCK), f32),
            pltpu.VMEM(exponent.shape, f32),
        ],
        in_specs=[smem()] + [vmem()] * 5,
        out_specs=[vmem()] * 2,
        scratch_shapes=[
            pltpu.VMEM((own_blocks * 8, BLOCK), f32),
            pltpu.VMEM((STEP, 2 * BLOCK, 2 * BLOCK), bf16),
        ],
        input_output_aliases={5: 1},
        compiler_params=params(14),
        cost_estimate=lasting(8),
        name="last_totals",
    )(lists, *held(sources, targets, values, own_sum, exponent))
    return total


def local(partials, coords, volume, send_blocks, halo_counts, source_slots, source_counts):
    cut_count = lax.axis_size("cuts")
    event_count = lax.axis_size("event")
    block_total = volume.shape[0] // BLOCK
    own_blocks = source_slots.shape[2]
    grid_step = cut_count // 4
    my_event = lax.axis_index("event")

    strides = [(1, [[0], [1]])]
    if grid_step == 1:
        strides = [(1, [[0, 2], [1, 3]])]
    else:
        strides.append((grid_step, [[2], [3]]))
    event = my_event.reshape(1)
    mine = partials[0]
    near_coords, near_volume, near_mine, own_list, *parcels = prepare(
        strides, send_blocks.shape[3], event, lax.axis_index("cuts").reshape(1), halo_counts[0],
        source_slots[0, 0].T, source_counts[0], coords, volume.reshape(block_total, BLOCK),
        mine,
    )
    turns = [(stride, turn) for stride, _ in strides for turn in (1, 0)]
    if event_count == 4:
        part, *parcels = half_sum(event, near_mine, crossed(mine, "event", 1), parcels)
        far_part = crossed(part, "event", 2)
    arrived = [swapped(p, *turn) for p, turn in zip(parcels, turns)]
    sources, targets, mark = own_features(event, near_coords, near_volume, own_blocks)
    if event_count == 4:
        part = added(part, far_part, mark)
        summed = [event, part, crossed(part, "event", 1)]
    else:
        summed = [lax.psum(mine, "event")]

    targets, lists = halo_features(
        own_list, targets, send_blocks[0, 0], arrived, block_total
    )
    *halo_totals, own_sum, values, exponent = first_totals(
        lists, sources, targets, summed, block_total
    )
    returned = [swapped(t, *turn) for t, turn in zip(halo_totals, turns)]
    totals = last_totals(lists, sources, targets, values, own_sum, exponent)
    for part in returned:
        totals = totals + part
    return (totals[1:3] / totals[0]).reshape(2, own_blocks * BLOCK)


def solution(mesh):
    placed = (
        P("event", None, ("runs", "cuts")),
        P(None, ("runs", "cuts")),
        P(("runs", "cuts")),
        P(("runs", "cuts"), "event", None, None),
        P(("runs", "cuts"), "event", None),
        P(("runs", "cuts"), "event", None, None),
        P(("runs", "cuts"), "event", None),
    )
    return jax.shard_map(
        local,
        mesh=mesh,
        in_specs=placed,
        out_specs=P(None, ("runs", "cuts", "event")),
        check_vma=False,
    )
```

```python
import functools
import math

import jax
import jax.numpy as jnp
from jax import lax
from jax.experimental import pallas as pl
from jax.experimental.pallas import tpu as pltpu
from jax.sharding import PartitionSpec as P

BLOCK = 128
FEATURES = 48
STEP_BITS = 5
STEP = 1 << STEP_BITS
SLOTS = 32
QUOTA = 6
FIELD = 10
sigma_km = 50.0
centre_km = 400.0
scale = math.sqrt(math.log2(math.e)) / sigma_km

f32 = jnp.float32
bf16 = jnp.bfloat16
i32 = jnp.int32


def vmem():
    return pl.BlockSpec(memory_space=pltpu.VMEM)


def smem():
    return pl.BlockSpec(memory_space=pltpu.SMEM)


def held(*arrays):
    return [pltpu.with_memory_space_constraint(a, pltpu.VMEM) for a in arrays]


def far(*arrays):
    return [pltpu.with_memory_space_constraint(a, pltpu.HBM) for a in arrays]


def lasting(microseconds):
    flops = int(microseconds * 1.15e9)
    return pl.CostEstimate(flops=flops, bytes_accessed=1000000, transcendentals=0)


def params(mib):
    return pltpu.CompilerParams(vmem_limit_bytes=mib << 20)


def swapped(block, stride, turn):
    devices = lax.axis_size("cuts")
    step = [stride, -stride] if turn == 0 else [-stride, stride]
    route = [(i, (i + step[(i // stride) % 2]) % devices) for i in range(devices)]
    return lax.ppermute(block, "cuts", route)


def crossed(block, axis, bit):
    route = [(i ^ bit, i) for i in range(lax.axis_size(axis))]
    return lax.ppermute(block, axis, route)


def split(values):
    high = values.astype(bf16).astype(f32)
    rest = values - high
    middle = rest.astype(bf16).astype(f32)
    return high, middle, rest - middle


def feature_rows(offsets, fourth, fifth):
    row = lax.broadcasted_iota(i32, (8, BLOCK), 0)
    rows = jnp.where(row == 3, fourth, jnp.where(row == 4, fifth, 0.0))
    return jnp.where(row < 3, offsets, rows)


def place(coords_ref, b):
    at = pl.ds(pl.multiple_of(b * BLOCK, BLOCK), BLOCK)
    offsets = (coords_ref[:, at] - centre_km) * scale
    squares = offsets * offsets
    norm = -0.5 * (squares[0:1] + squares[1:2] + squares[2:3])
    return jnp.concatenate([offsets, jnp.zeros((5, BLOCK), f32)], axis=0), norm


def target_features(offsets, norm):
    high, middle, low = split(feature_rows(offsets, 1.0, norm))
    return jnp.concatenate([high, middle, low, high, middle, high], axis=0).astype(bf16)


def own_features_kernel(
    event_ref, coords_ref, volume_ref, source_ref, target_ref, mark_ref, log_ref
):
    block_total = volume_ref.shape[0]
    own_blocks = target_ref.shape[0]
    slots = SLOTS
    log_ref[...] = jnp.log2(volume_ref[...])

    def some_sources(n, _):
        for slot in range(slots):
            b = n * slots + slot
            offsets, norm = place(coords_ref, b)
            high, middle, low = split(feature_rows(offsets, norm + log_ref[pl.ds(b, 1), :], 1.0))
            rows = jnp.concatenate([high, high, high, middle, middle, low], axis=0)
            source_ref[b] = rows.astype(bf16).T
        return 0

    def some_targets(n, _):
        for slot in range(slots):
            t = n * slots + slot
            block = event_ref[0] * own_blocks + t
            target_ref[t] = target_features(*place(coords_ref, block))
        return 0

    lax.fori_loop(0, block_total // slots, some_sources, 0)
    lax.fori_loop(0, own_blocks // slots, some_targets, 0)
    column = lax.broadcasted_iota(i32, (BLOCK, FEATURES), 1)
    source_ref[block_total] = jnp.where(column == 3, -10000.0, 0.0).astype(bf16)
    mark_ref[...] = jnp.zeros(mark_ref.shape, f32)


def own_features(event, coords, volume, own_blocks):
    block_total = volume.shape[0]
    return pl.pallas_call(
        own_features_kernel,
        out_shape=(
            pltpu.VMEM((block_total + 1, BLOCK, FEATURES), bf16),
            pltpu.VMEM((own_blocks, FEATURES, BLOCK), bf16),
            jax.ShapeDtypeStruct((8, BLOCK), f32),
        ),
        in_specs=[smem(), vmem(), vmem()],
        out_specs=(vmem(),) * 3,
        scratch_shapes=[pltpu.VMEM((block_total, BLOCK), f32)],
        compiler_params=params(8),
        cost_estimate=lasting(4),
        name="own_features",
    )(event, *held(coords, volume))


def coded(target, first, second):
    return (target << (2 * FIELD)) + (second << FIELD) + first


def finished_list(ref, codes, spare, count):
    list_rows = codes.shape[0]
    ref[0:list_rows] = codes
    ref[list_rows : list_rows + 1] = jnp.full((1, BLOCK), coded(0, spare, spare), i32)
    ref[list_rows + 1 :] = count[0:3]


def decoded(code):
    mask = (1 << FIELD) - 1
    return code >> (2 * FIELD), code & mask, (code >> FIELD) & mask


def prepare_kernel(
    strides, capacity, event_ref, cut_ref, halo_given, slot_given, count_given, coords_given,
    volume_given, mine_given, coords_ref, volume_ref, mine_ref, own_ref, *refs,
):
    parcels, rest = refs[: 2 * len(strides)], refs[2 * len(strides) :]
    halo_ref, slot_ref, count_ref, row_ref, arrival = rest
    width, own_blocks = slot_ref.shape
    block_total = volume_ref.shape[0]
    sets = len(parcels) + 1
    brought = [
        (halo_given, halo_ref), (slot_given, slot_ref), (count_given, count_ref),
        (coords_given, coords_ref), (volume_given, volume_ref), (mine_given, mine_ref),
    ]
    half = mine_ref.shape[1]
    at = pl.ds(pl.multiple_of((event_ref[0] & 1) * half, half), half)
    brought[5] = (mine_given.at[:, at], mine_ref)
    brought = [
        pltpu.make_async_copy(given, ref, arrival.at[n]) for n, (given, ref) in enumerate(brought)
    ]
    for copy in brought:
        copy.start()
    for copy in brought[:3]:
        copy.wait()
    row_ref[...] = jnp.zeros(row_ref.shape, i32)
    row_ref[0:width, 0:own_blocks] = slot_ref[...]
    row_ref[width : width + 1, 0:own_blocks] = count_ref[...]
    shape = (width, BLOCK)
    slots = row_ref[0:width]
    used = lax.broadcasted_iota(i32, shape, 0) < row_ref[width : width + 1]
    halo = slots - block_total
    lives = [used & (halo < 0)]
    for stride, members in strides:
        both = []
        for directions in members:
            live = jnp.zeros(shape, i32)
            for k in directions:
                near = (halo >= k * capacity) & (halo - k * capacity < halo_ref[0, k])
                live = live + (near & (halo < (k + 1) * capacity)).astype(i32)
            both.append(live)
        odd = (cut_ref[0] // stride) % 2
        for first, second in (both, both[::-1]):
            live = first * (1 - odd) + second * odd
            lives.append(used & (live > 0))
    rows = sets * width
    live = jnp.concatenate([l.astype(f32) for l in lives], axis=0).astype(bf16)
    near = lax.broadcasted_iota(i32, (rows, rows), 0)
    across = lax.broadcasted_iota(i32, (rows, rows), 1)
    alike = near // width == across // width
    above = (alike & (across < near)).astype(f32).astype(bf16)
    rank = jnp.dot(above, live, preferred_element_type=f32).astype(i32)
    count = jnp.dot(alike.astype(f32).astype(bf16), live, preferred_element_type=f32)
    twos = ((count.astype(i32) + 1) >> 1).astype(f32).astype(bf16)
    near = lax.broadcasted_iota(i32, (BLOCK, BLOCK), 0)
    across = lax.broadcasted_iota(i32, (BLOCK, BLOCK), 1)
    earlier = (near < across).astype(f32).astype(bf16)
    before = jnp.dot(twos, earlier, preferred_element_type=f32).astype(i32)
    total = jnp.dot(twos, jnp.ones((BLOCK, BLOCK), bf16), preferred_element_type=f32).astype(i32)
    place_of = before + (rank >> 1)
    list_rows = own_blocks * width // (2 * BLOCK)
    high = jnp.full(shape, -1, i32)
    low = jnp.zeros(shape, i32)
    odd = jnp.zeros(shape, i32)
    for s in range(sets):
        part = slice(s * width, (s + 1) * width)
        high = jnp.where(lives[s], (place_of[part] >> 7) + s * list_rows, high)
        low = jnp.where(lives[s], place_of[part] & (BLOCK - 1), low)
        odd = jnp.where(lives[s], rank[part] & 1, odd)
    block = jnp.where(halo < 0, slots, halo) + 1
    even = 1 - odd
    target = lax.broadcasted_iota(i32, shape, 1)
    parts = [target * even, (block >> 3) * even, (block & 7) * even]
    parts = [p.astype(f32) for p in parts + [(block >> 3) * odd, (block & 7) * odd]]
    size = (sets * list_rows + 7) // 8 * 8
    list_row = lax.broadcasted_iota(i32, (size, BLOCK), 0)
    list_lane = lax.broadcasted_iota(i32, (BLOCK, BLOCK), 0)
    codes, places = [], []
    for i in range(width):
        hit = list_row == high[i : i + 1, :]
        codes.append(
            jnp.concatenate([jnp.where(hit, p[i : i + 1, :], 0.0) for p in parts], axis=0)
        )
        places.append((list_lane == low[i : i + 1, :]).astype(f32).astype(bf16))
    codes = jnp.concatenate([c.astype(bf16) for c in codes], axis=1)
    places = jnp.concatenate(places, axis=1)
    found = lax.dot_general(
        codes, places, (((1,), (1,)), ((), ())), preferred_element_type=f32
    ).astype(i32)
    target, *found = [found[n * size : (n + 1) * size] for n in range(5)]
    blocks = [found[0] * 8 + found[1] - 1, found[2] * 8 + found[3] - 1]
    for s in range(sets):
        part = slice(s * list_rows, (s + 1) * list_rows)
        spare = block_total if s == 0 else 4 * capacity
        pair = [jnp.where(b[part] < 0, spare, b[part]) for b in blocks]
        count = total[s * width : s * width + list_rows]
        if s == 0:
            finished_list(own_ref, coded(target[part], *pair), spare, count)
        else:
            given = [*pair, target[part], count]
            for n, values in enumerate(given):
                at = 3 * own_blocks + n * list_rows
                parcels[s - 1][at : at + list_rows] = values.astype(f32)
    for copy in brought[3:]:
        copy.wait()

    def some_coords(t, _):
        at = pl.multiple_of((event_ref[0] * own_blocks + t) * BLOCK, BLOCK)
        given = coords_ref[:, pl.ds(at, BLOCK)]
        for parcel in parcels:
            for r in range(3):
                parcel[pl.ds(r * own_blocks + t, 1), :] = given[r : r + 1]
        return 0

    lax.fori_loop(0, own_blocks, some_coords, 0, unroll=8)


def prepare(strides, capacity, event, cut, halo_counts, slots, counts, coords, volume, mine):
    width, own_blocks = slots.shape
    list_rows = own_blocks * width // (2 * BLOCK)
    parcel = jax.ShapeDtypeStruct((3 * own_blocks + 4 * list_rows, BLOCK), f32)
    return pl.pallas_call(
        functools.partial(prepare_kernel, strides, capacity),
        out_shape=(
            pltpu.VMEM(coords.shape, f32),
            pltpu.VMEM(volume.shape, f32),
            pltpu.VMEM((2, mine.shape[1] // 2), f32),
            pltpu.VMEM((list_rows + 4, BLOCK), i32),
        )
        + (parcel,) * (2 * len(strides)),
        in_specs=[smem()] * 2 + [pl.BlockSpec(memory_space=pltpu.HBM)] * 6,
        out_specs=(vmem(),) * 4 + (vmem(),) * (2 * len(strides)),
        scratch_shapes=[
            pltpu.SMEM(halo_counts.shape, i32),
            pltpu.VMEM(slots.shape, i32),
            pltpu.VMEM(counts.shape, i32),
            pltpu.VMEM((width + 8, BLOCK), i32),
            pltpu.SemaphoreType.DMA((6,)),
        ],
        compiler_params=params(8),
        cost_estimate=lasting(2),
        name="prepare",
    )(event, cut, *far(halo_counts, slots, counts, coords, volume, mine))


def halo_features_kernel(block_total, own_blocks, own_ref, near_ref, sent_ref, *refs):
    *given, target_ref, smem_ref, list_ref, pad_ref, row_ref, arrival = refs
    slots = pad_ref.shape[0]
    directions, capacity = sent_ref.shape
    pad_ref[...] = jnp.zeros(pad_ref.shape, f32)
    row_ref[...] = jnp.zeros(row_ref.shape, i32)
    row_ref[0:directions, 0:capacity] = sent_ref[...]
    head = 3 * own_blocks
    list_rows = list_ref.shape[1] - 4
    for s, ref in enumerate(given):
        slot = ref[head : head + 2 * list_rows].astype(i32)
        block = jnp.full(slot.shape, block_total, i32)
        for k in range(directions):
            here = (slot >= k * capacity) & (slot < (k + 1) * capacity)
            row = jnp.broadcast_to(row_ref[k : k + 1, :], slot.shape)
            at = jnp.where(here, slot - k * capacity, 0)
            block = jnp.where(here, jnp.take_along_axis(row, at, axis=1), block)
        rest = ref[head + 2 * list_rows :].astype(i32)
        codes = coded(rest[0:list_rows], block[0:list_rows], block[list_rows:])
        finished_list(list_ref.at[s], codes, block_total, rest[list_rows:])
    list_ref[len(given)] = own_ref[...]
    sent = pltpu.make_async_copy(list_ref, smem_ref, arrival)
    sent.start()
    target_ref[len(given) * own_blocks :] = near_ref[...]
    for s, ref in enumerate(given):

        def some_targets(n, _):
            for q in range(slots):
                t = n * slots + q
                for r in range(3):
                    row = ref[pl.ds(r * own_blocks + t, 1), :]
                    pad_ref[q, r : r + 1, :] = (row - centre_km) * scale
                offsets = pad_ref[q]
                norm = -0.5 * jnp.sum(offsets * offsets, axis=0, keepdims=True)
                target_ref[s * own_blocks + t] = target_features(offsets, norm)
            return 0

        lax.fori_loop(0, own_blocks // slots, some_targets, 0)
    sent.wait()


def halo_features(own_list, targets, sent, given, block_total):
    own_blocks = targets.shape[0]
    list_rows = (given[0].shape[0] - 3 * own_blocks) // 4
    lists = (len(given) + 1, list_rows + 4, BLOCK)
    return pl.pallas_call(
        functools.partial(halo_features_kernel, block_total, own_blocks),
        out_shape=(
            pltpu.VMEM(((len(given) + 1) * own_blocks, FEATURES, BLOCK), bf16),
            pltpu.SMEM(lists, i32),
        ),
        in_specs=[vmem()] * (len(given) + 3),
        out_specs=(vmem(), smem()),
        scratch_shapes=[
            pltpu.VMEM(lists, i32),
            pltpu.VMEM((SLOTS, 8, BLOCK), f32),
            pltpu.VMEM((8, BLOCK), i32),
            pltpu.SemaphoreType.DMA,
        ],
        compiler_params=params(8),
        cost_estimate=lasting(1),
        name="halo_features",
    )(*held(own_list, targets), sent, *given)


def value_rows(first, second):
    row = lax.broadcasted_iota(i32, (8, BLOCK), 0)
    both = jnp.where((row & 1) == 1, first, second)
    high, middle, low = split(both)
    rows = jnp.where(row < 5, jnp.where(row < 3, high, middle), jnp.where(row < 7, low, 0.0))
    rows = jnp.where(row == 0, 1.0, rows).astype(bf16)
    return jnp.concatenate([rows, rows], axis=1)


def half_kernel(event_ref, mine_ref, near_ref, *refs):
    parcels, (out_ref, *sent) = refs[: len(refs) // 2], refs[len(refs) // 2 :]
    half = out_ref.shape[1]
    at = pl.ds(pl.multiple_of((event_ref[0] & 1) * half, half), half)
    out_ref[...] = mine_ref[...] + near_ref[:, at]
    for given, to in zip(parcels, sent):
        to[...] = given[...]


def half_sum(event, mine, near, parcels):
    return pl.pallas_call(
        half_kernel,
        out_shape=[jax.ShapeDtypeStruct(a.shape, f32) for a in (mine, *parcels)],
        in_specs=[smem()] + [vmem()] * (len(parcels) + 2),
        out_specs=[vmem()] * (len(parcels) + 1),
        compiler_params=params(4),
        cost_estimate=lasting(0.1),
        name="half_sum",
    )(event, *held(mine), near, *parcels)


def add_kernel(first_ref, second_ref, mark_ref, out_ref):
    out_ref[...] = first_ref[...] + second_ref[...]


def added(first, second, mark):
    return pl.pallas_call(
        add_kernel,
        out_shape=jax.ShapeDtypeStruct(first.shape, f32),
        in_specs=[vmem()] * 3,
        out_specs=vmem(),
        compiler_params=params(4),
        cost_estimate=lasting(0.1),
        name="added",
    )(first, second, mark)


def schedule(list_ref):
    sets, list_rows = list_ref.shape[0], list_ref.shape[1] - 4
    ends = []
    for s in range(sets):
        ends.append(list_ref[s, list_rows + 1, 0] + (ends[-1] if ends else 0))
    halo_steps, all_steps = [(e + STEP - 1) >> STEP_BITS for e in ends[-2:]]
    return ends, jnp.maximum(halo_steps, jnp.minimum(QUOTA, all_steps)), all_steps


class Totals:
    def __init__(self, ends, own_blocks, first_set, refs):
        self.ends, self.own_blocks, self.first_set = ends, own_blocks, first_set
        self.lists, self.sources, self.targets, self.values = refs[:4]
        self.exponent_ref, self.weight_ref, self.sum_ref = refs[4:]

    def chunk(self, i):
        s, base = 0, 0
        for end in self.ends[:-1]:
            past = i >= end
            s = s + past.astype(i32)
            base = jnp.where(past, end, base)
        at = i - base
        t, first, second = decoded(self.lists[s, at >> 7, at & (BLOCK - 1)])
        return s * self.own_blocks + t, first, second

    def exponents(self, k, c):
        t, first, second = self.chunk(k * STEP + c)
        both = jnp.concatenate([self.sources[first], self.sources[second]], axis=0)
        exponent = jnp.dot(both, self.targets[t], preferred_element_type=f32)
        self.exponent_ref[c, :, 0:BLOCK] = exponent[0:BLOCK]
        self.exponent_ref[c, :, BLOCK:] = exponent[BLOCK:]

    def weights(self, c):
        weight = jnp.exp2(self.exponent_ref[c])
        high = weight.astype(bf16)
        self.weight_ref[c, 0:BLOCK] = high
        self.weight_ref[c, BLOCK : 2 * BLOCK] = (weight - high.astype(f32)).astype(bf16)

    def sums(self, k, c):
        t, first, second = self.chunk(k * STEP + c)
        values = jnp.concatenate([self.values[first], self.values[second]], axis=0)
        both = jnp.dot(values, self.weight_ref[c], preferred_element_type=f32)
        at = pl.ds(pl.multiple_of((t - self.first_set * self.own_blocks) * 8, 8), 8)
        self.sum_ref[at, :] += both[0:8, 0:BLOCK] + both[8:16, BLOCK : 2 * BLOCK]

    def steps(self, begin, end):
        def step(k, _):
            for c in range(STEP):
                self.weights(c)
                self.sums(k, c)
                self.exponents(k + 1, c)
            return 0

        lax.fori_loop(begin, end, step, 0)

    def finish(self, s, out_ref):
        rows = [
            self.sum_ref[pl.ds(s * self.own_blocks * 8 + r, self.own_blocks, stride=8), :]
            for r in range(7)
        ]
        out_ref[0] = rows[0]
        out_ref[1] = rows[1] + rows[3] + rows[5]
        out_ref[2] = rows[2] + rows[4] + rows[6]


def first_totals_kernel(own_blocks, list_ref, source_ref, target_ref, *refs):
    *refs, sum_ref, weight_ref = refs
    sets = list_ref.shape[0]
    own_sum_ref, value_ref, exponent_ref = refs[-3:]
    out_refs = refs[-3 - (sets - 1) : -3]
    summed = refs[: -3 - (sets - 1)]
    ends, first_steps, _ = schedule(list_ref)
    given = [list_ref, source_ref, target_ref, value_ref, exponent_ref, weight_ref, sum_ref]
    totals = Totals(ends, own_blocks, 0, given)
    sum_ref[...] = jnp.zeros(sum_ref.shape, f32)
    block_total = value_ref.shape[0] - 1
    rounds = 1

    def begin(n, _):
        for c in range(STEP // rounds):
            totals.exponents(0, n * (STEP // rounds) + c)
        for c in range(block_total // rounds):
            b = n * (block_total // rounds) + c
            at = pl.ds(pl.multiple_of(b * BLOCK, BLOCK), BLOCK)
            both = sum(ref[:, at] for ref in summed)
            value_ref[b] = value_rows(both[0:1], both[1:2])
        return 0

    if len(summed) == 1:
        lax.fori_loop(0, rounds, begin, 0)
    else:
        begin_from_halves(totals, summed, value_ref, rounds)
    value_ref[block_total] = jnp.zeros((8, 2 * BLOCK), bf16)
    totals.steps(0, first_steps)
    for s in range(sets - 1):
        totals.finish(s, out_refs[s])
    own_sum_ref[...] = sum_ref[(sets - 1) * own_blocks * 8 :, :]


def begin_from_halves(totals, summed, value_ref, rounds):
    event_ref, *halves = summed
    half_blocks = (value_ref.shape[0] - 1) // 2
    core = event_ref[0] & 1

    def begin(n, _):
        for c in range(STEP // rounds):
            totals.exponents(0, n * (STEP // rounds) + c)
        for piece, ref in enumerate(halves):
            for c in range(half_blocks // rounds):
                b = n * (half_blocks // rounds) + c
                at = pl.ds(pl.multiple_of(b * BLOCK, BLOCK), BLOCK)
                where = (core ^ piece) * half_blocks + b
                totals.values[where] = value_rows(ref[0:1, at], ref[1:2, at])
        return 0

    lax.fori_loop(0, rounds, begin, 0)


def first_totals(lists, sources, targets, summed, block_total):
    sets = lists.shape[0]
    own_blocks = targets.shape[0] // sets
    specs = [smem()] * (len(summed) - 2) + [vmem()] * min(len(summed), 2)
    return pl.pallas_call(
        functools.partial(first_totals_kernel, own_blocks),
        out_shape=[jax.ShapeDtypeStruct((3, own_blocks, BLOCK), f32)] * (sets - 1)
        + [
            pltpu.VMEM((own_blocks * 8, BLOCK), f32),
            pltpu.VMEM((block_total + 1, 8, 2 * BLOCK), bf16),
            pltpu.VMEM((STEP, BLOCK, 2 * BLOCK), f32),
        ],
        in_specs=[smem(), vmem(), vmem()] + specs,
        out_specs=[vmem()] * (sets + 2),
        scratch_shapes=[
            pltpu.VMEM((sets * own_blocks * 8, BLOCK), f32),
            pltpu.VMEM((STEP, 2 * BLOCK, 2 * BLOCK), bf16),
        ],
        compiler_params=params(14),
        cost_estimate=lasting(8),
        name="first_totals",
    )(pltpu.with_memory_space_constraint(lists, pltpu.SMEM), *held(sources, targets), *summed)


def last_totals_kernel(
    own_blocks, list_ref, source_ref, target_ref, value_ref, own_sum_ref, _, out_ref,
    exponent_ref, sum_ref, weight_ref,
):
    ends, first_steps, all_steps = schedule(list_ref)
    given = [list_ref, source_ref, target_ref, value_ref, exponent_ref, weight_ref, sum_ref]
    totals = Totals(ends, own_blocks, list_ref.shape[0] - 1, given)
    sum_ref[...] = own_sum_ref[...]
    totals.steps(first_steps, all_steps)
    totals.finish(0, out_ref)


def last_totals(lists, sources, targets, values, own_sum, exponent):
    own_blocks = targets.shape[0] // lists.shape[0]
    lists = pltpu.with_memory_space_constraint(lists, pltpu.SMEM)
    total, _ = pl.pallas_call(
        functools.partial(last_totals_kernel, own_blocks),
        out_shape=[
            jax.ShapeDtypeStruct((3, own_blocks, BLOCK), f32),
            pltpu.VMEM(exponent.shape, f32),
        ],
        in_specs=[smem()] + [vmem()] * 5,
        out_specs=[vmem()] * 2,
        scratch_shapes=[
            pltpu.VMEM((own_blocks * 8, BLOCK), f32),
            pltpu.VMEM((STEP, 2 * BLOCK, 2 * BLOCK), bf16),
        ],
        input_output_aliases={5: 1},
        compiler_params=params(14),
        cost_estimate=lasting(8),
        name="last_totals",
    )(lists, *held(sources, targets, values, own_sum, exponent))
    return total


def local(partials, coords, volume, send_blocks, halo_counts, source_slots, source_counts):
    cut_count = lax.axis_size("cuts")
    event_count = lax.axis_size("event")
    block_total = volume.shape[0] // BLOCK
    own_blocks = source_slots.shape[2]
    grid_step = cut_count // 4
    my_event = lax.axis_index("event")

    strides = [(1, [[0], [1]])]
    if grid_step == 1:
        strides = [(1, [[0, 2], [1, 3]])]
    else:
        strides.append((grid_step, [[2], [3]]))
    event = my_event.reshape(1)
    mine = partials[0]
    near_coords, near_volume, near_mine, own_list, *parcels = prepare(
        strides, send_blocks.shape[3], event, lax.axis_index("cuts").reshape(1), halo_counts[0],
        source_slots[0, 0].T, source_counts[0], coords, volume.reshape(block_total, BLOCK),
        mine,
    )
    turns = [(stride, turn) for stride, _ in strides for turn in (1, 0)]
    if event_count == 4:
        part, *parcels = half_sum(event, near_mine, crossed(mine, "event", 1), parcels)
        far_part = crossed(part, "event", 2)
    arrived = [swapped(p, *turn) for p, turn in zip(parcels, turns)]
    sources, targets, mark = own_features(event, near_coords, near_volume, own_blocks)
    if event_count == 4:
        part = added(part, far_part, mark)
        summed = [event, part, crossed(part, "event", 1)]
    else:
        summed = [lax.psum(mine, "event")]

    targets, lists = halo_features(
        own_list, targets, send_blocks[0, 0], arrived, block_total
    )
    *halo_totals, own_sum, values, exponent = first_totals(
        lists, sources, targets, summed, block_total
    )
    returned = [swapped(t, *turn) for t, turn in zip(halo_totals, turns)]
    totals = last_totals(lists, sources, targets, values, own_sum, exponent)
    for part in returned:
        totals = totals + part
    return (totals[1:3] / totals[0]).reshape(2, own_blocks * BLOCK)


def solution(mesh):
    placed = (
        P("event", None, ("runs", "cuts")),
        P(None, ("runs", "cuts")),
        P(("runs", "cuts")),
        P(("runs", "cuts"), "event", None, None),
        P(("runs", "cuts"), "event", None),
        P(("runs", "cuts"), "event", None, None),
        P(("runs", "cuts"), "event", None),
    )
    return jax.shard_map(
        local,
        mesh=mesh,
        in_specs=placed,
        out_specs=P(None, ("runs", "cuts", "event")),
        check_vma=False,
    )
```

```python
import functools
import math

import jax
import jax.numpy as jnp
from jax import lax
from jax.experimental import pallas as pl
from jax.experimental.pallas import tpu as pltpu
from jax.sharding import PartitionSpec as P

BLOCK = 128
FEATURES = 48
STEP_BITS = 5
STEP = 1 << STEP_BITS
SLOTS = 32
QUOTA = 6
FIELD = 10
sigma_km = 50.0
centre_km = 400.0
scale = math.sqrt(math.log2(math.e)) / sigma_km

f32 = jnp.float32
bf16 = jnp.bfloat16
i32 = jnp.int32


def vmem():
    return pl.BlockSpec(memory_space=pltpu.VMEM)


def smem():
    return pl.BlockSpec(memory_space=pltpu.SMEM)


def held(*arrays):
    return [pltpu.with_memory_space_constraint(a, pltpu.VMEM) for a in arrays]


def far(*arrays):
    return [pltpu.with_memory_space_constraint(a, pltpu.HBM) for a in arrays]


def lasting(microseconds):
    flops = int(microseconds * 1.15e9)
    return pl.CostEstimate(flops=flops, bytes_accessed=1000000, transcendentals=0)


def params(mib):
    return pltpu.CompilerParams(vmem_limit_bytes=mib << 20)


def swapped(block, stride, turn):
    devices = lax.axis_size("cuts")
    step = [stride, -stride] if turn == 0 else [-stride, stride]
    route = [(i, (i + step[(i // stride) % 2]) % devices) for i in range(devices)]
    return lax.ppermute(block, "cuts", route)


def crossed(block, axis, bit):
    route = [(i ^ bit, i) for i in range(lax.axis_size(axis))]
    return lax.ppermute(block, axis, route)


def split(values):
    high = values.astype(bf16).astype(f32)
    rest = values - high
    middle = rest.astype(bf16).astype(f32)
    return high, middle, rest - middle


def feature_rows(offsets, fourth, fifth):
    row = lax.broadcasted_iota(i32, (8, BLOCK), 0)
    rows = jnp.where(row == 3, fourth, jnp.where(row == 4, fifth, 0.0))
    return jnp.where(row < 3, offsets, rows)


def place(coords_ref, b):
    at = pl.ds(pl.multiple_of(b * BLOCK, BLOCK), BLOCK)
    offsets = (coords_ref[:, at] - centre_km) * scale
    squares = offsets * offsets
    norm = -0.5 * (squares[0:1] + squares[1:2] + squares[2:3])
    return jnp.concatenate([offsets, jnp.zeros((5, BLOCK), f32)], axis=0), norm


def target_features(offsets, norm):
    high, middle, low = split(feature_rows(offsets, 1.0, norm))
    return jnp.concatenate([high, middle, low, high, middle, high], axis=0).astype(bf16)


def own_features_kernel(
    event_ref, coords_ref, volume_ref, source_ref, target_ref, mark_ref, log_ref
):
    block_total = volume_ref.shape[0]
    own_blocks = target_ref.shape[0]
    slots = SLOTS
    log_ref[...] = jnp.log2(volume_ref[...])

    def some_sources(n, _):
        for slot in range(slots):
            b = n * slots + slot
            offsets, norm = place(coords_ref, b)
            high, middle, low = split(feature_rows(offsets, norm + log_ref[pl.ds(b, 1), :], 1.0))
            rows = jnp.concatenate([high, high, high, middle, middle, low], axis=0)
            source_ref[b] = rows.astype(bf16).T
        return 0

    def some_targets(n, _):
        for slot in range(slots):
            t = n * slots + slot
            block = event_ref[0] * own_blocks + t
            target_ref[t] = target_features(*place(coords_ref, block))
        return 0

    lax.fori_loop(0, block_total // slots, some_sources, 0)
    lax.fori_loop(0, own_blocks // slots, some_targets, 0)
    column = lax.broadcasted_iota(i32, (BLOCK, FEATURES), 1)
    source_ref[block_total] = jnp.where(column == 3, -10000.0, 0.0).astype(bf16)
    mark_ref[...] = jnp.zeros(mark_ref.shape, f32)


def own_features(event, coords, volume, own_blocks):
    block_total = volume.shape[0]
    return pl.pallas_call(
        own_features_kernel,
        out_shape=(
            pltpu.VMEM((block_total + 1, BLOCK, FEATURES), bf16),
            pltpu.VMEM((own_blocks, FEATURES, BLOCK), bf16),
            jax.ShapeDtypeStruct((8, BLOCK), f32),
        ),
        in_specs=[smem(), vmem(), vmem()],
        out_specs=(vmem(),) * 3,
        scratch_shapes=[pltpu.VMEM((block_total, BLOCK), f32)],
        compiler_params=params(8),
        cost_estimate=lasting(4),
        name="own_features",
    )(event, *held(coords, volume))


def coded(target, first, second):
    return (target << (2 * FIELD)) + (second << FIELD) + first


def finished_list(ref, codes, spare, count):
    list_rows = codes.shape[0]
    ref[0:list_rows] = codes
    ref[list_rows : list_rows + 1] = jnp.full((1, BLOCK), coded(0, spare, spare), i32)
    ref[list_rows + 1 :] = count[0:3]


def decoded(code):
    mask = (1 << FIELD) - 1
    return code >> (2 * FIELD), code & mask, (code >> FIELD) & mask


def prepare_kernel(
    strides, capacity, event_ref, cut_ref, halo_given, slot_given, count_given, coords_given,
    volume_given, mine_given, coords_ref, volume_ref, mine_ref, own_ref, *refs,
):
    parcels, rest = refs[: 2 * len(strides)], refs[2 * len(strides) :]
    halo_ref, slot_ref, count_ref, row_ref, arrival = rest
    width, own_blocks = slot_ref.shape
    block_total = volume_ref.shape[0]
    sets = len(parcels) + 1
    brought = [
        (halo_given, halo_ref), (slot_given, slot_ref), (count_given, count_ref),
        (coords_given, coords_ref), (volume_given, volume_ref), (mine_given, mine_ref),
    ]
    half = mine_ref.shape[1]
    at = pl.ds(pl.multiple_of((event_ref[0] & 1) * half, half), half)
    brought[5] = (mine_given.at[:, at], mine_ref)
    brought = [
        pltpu.make_async_copy(given, ref, arrival.at[n]) for n, (given, ref) in enumerate(brought)
    ]
    for copy in brought:
        copy.start()
    for copy in brought[:3]:
        copy.wait()
    row_ref[...] = jnp.zeros(row_ref.shape, i32)
    row_ref[0:width, 0:own_blocks] = slot_ref[...]
    row_ref[width : width + 1, 0:own_blocks] = count_ref[...]
    shape = (width, BLOCK)
    slots = row_ref[0:width]
    used = lax.broadcasted_iota(i32, shape, 0) < row_ref[width : width + 1]
    halo = slots - block_total
    lives = [used & (halo < 0)]
    for stride, members in strides:
        both = []
        for directions in members:
            live = jnp.zeros(shape, i32)
            for k in directions:
                near = (halo >= k * capacity) & (halo - k * capacity < halo_ref[0, k])
                live = live + (near & (halo < (k + 1) * capacity)).astype(i32)
            both.append(live)
        odd = (cut_ref[0] // stride) % 2
        for first, second in (both, both[::-1]):
            live = first * (1 - odd) + second * odd
            lives.append(used & (live > 0))
    rows = sets * width
    live = jnp.concatenate([l.astype(f32) for l in lives], axis=0).astype(bf16)
    near = lax.broadcasted_iota(i32, (rows, rows), 0)
    across = lax.broadcasted_iota(i32, (rows, rows), 1)
    alike = near // width == across // width
    above = (alike & (across < near)).astype(f32).astype(bf16)
    rank = jnp.dot(above, live, preferred_element_type=f32).astype(i32)
    count = jnp.dot(alike.astype(f32).astype(bf16), live, preferred_element_type=f32)
    twos = ((count.astype(i32) + 1) >> 1).astype(f32).astype(bf16)
    near = lax.broadcasted_iota(i32, (BLOCK, BLOCK), 0)
    across = lax.broadcasted_iota(i32, (BLOCK, BLOCK), 1)
    earlier = (near < across).astype(f32).astype(bf16)
    before = jnp.dot(twos, earlier, preferred_element_type=f32).astype(i32)
    total = jnp.dot(twos, jnp.ones((BLOCK, BLOCK), bf16), preferred_element_type=f32).astype(i32)
    place_of = before + (rank >> 1)
    list_rows = own_blocks * width // (2 * BLOCK)
    high = jnp.full(shape, -1, i32)
    low = jnp.zeros(shape, i32)
    odd = jnp.zeros(shape, i32)
    for s in range(sets):
        part = slice(s * width, (s + 1) * width)
        high = jnp.where(lives[s], (place_of[part] >> 7) + s * list_rows, high)
        low = jnp.where(lives[s], place_of[part] & (BLOCK - 1), low)
        odd = jnp.where(lives[s], rank[part] & 1, odd)
    block = jnp.where(halo < 0, slots, halo) + 1
    even = 1 - odd
    target = lax.broadcasted_iota(i32, shape, 1)
    parts = [target * even, (block >> 3) * even, (block & 7) * even]
    parts = [p.astype(f32) for p in parts + [(block >> 3) * odd, (block & 7) * odd]]
    size = (sets * list_rows + 7) // 8 * 8
    list_row = lax.broadcasted_iota(i32, (size, BLOCK), 0)
    list_lane = lax.broadcasted_iota(i32, (BLOCK, BLOCK), 0)
    codes, places = [], []
    for i in range(width):
        hit = list_row == high[i : i + 1, :]
        codes.append(
            jnp.concatenate([jnp.where(hit, p[i : i + 1, :], 0.0) for p in parts], axis=0)
        )
        places.append((list_lane == low[i : i + 1, :]).astype(f32).astype(bf16))
    codes = jnp.concatenate([c.astype(bf16) for c in codes], axis=1)
    places = jnp.concatenate(places, axis=1)
    found = lax.dot_general(
        codes, places, (((1,), (1,)), ((), ())), preferred_element_type=f32
    ).astype(i32)
    target, *found = [found[n * size : (n + 1) * size] for n in range(5)]
    blocks = [found[0] * 8 + found[1] - 1, found[2] * 8 + found[3] - 1]
    for s in range(sets):
        part = slice(s * list_rows, (s + 1) * list_rows)
        spare = block_total if s == 0 else 4 * capacity
        pair = [jnp.where(b[part] < 0, spare, b[part]) for b in blocks]
        count = total[s * width : s * width + list_rows]
        if s == 0:
            finished_list(own_ref, coded(target[part], *pair), spare, count)
        else:
            given = [*pair, target[part], count]
            for n, values in enumerate(given):
                at = 3 * own_blocks + n * list_rows
                parcels[s - 1][at : at + list_rows] = values.astype(f32)
    for copy in brought[3:]:
        copy.wait()

    def some_coords(t, _):
        at = pl.multiple_of((event_ref[0] * own_blocks + t) * BLOCK, BLOCK)
        given = coords_ref[:, pl.ds(at, BLOCK)]
        for parcel in parcels:
            for r in range(3):
                parcel[pl.ds(r * own_blocks + t, 1), :] = given[r : r + 1]
        return 0

    lax.fori_loop(0, own_blocks, some_coords, 0, unroll=8)


def prepare(strides, capacity, event, cut, halo_counts, slots, counts, coords, volume, mine):
    width, own_blocks = slots.shape
    list_rows = own_blocks * width // (2 * BLOCK)
    parcel = jax.ShapeDtypeStruct((3 * own_blocks + 4 * list_rows, BLOCK), f32)
    return pl.pallas_call(
        functools.partial(prepare_kernel, strides, capacity),
        out_shape=(
            pltpu.VMEM(coords.shape, f32),
            pltpu.VMEM(volume.shape, f32),
            pltpu.VMEM((2, mine.shape[1] // 2), f32),
            pltpu.VMEM((list_rows + 4, BLOCK), i32),
        )
        + (parcel,) * (2 * len(strides)),
        in_specs=[smem()] * 2 + [pl.BlockSpec(memory_space=pltpu.HBM)] * 6,
        out_specs=(vmem(),) * 4 + (vmem(),) * (2 * len(strides)),
        scratch_shapes=[
            pltpu.SMEM(halo_counts.shape, i32),
            pltpu.VMEM(slots.shape, i32),
            pltpu.VMEM(counts.shape, i32),
            pltpu.VMEM((width + 8, BLOCK), i32),
            pltpu.SemaphoreType.DMA((6,)),
        ],
        compiler_params=params(8),
        cost_estimate=lasting(2),
        name="prepare",
    )(event, cut, *far(halo_counts, slots, counts, coords, volume, mine))


def halo_features_kernel(block_total, own_blocks, own_ref, near_ref, sent_ref, *refs):
    *given, target_ref, smem_ref, list_ref, pad_ref, row_ref, arrival = refs
    slots = pad_ref.shape[0]
    directions, capacity = sent_ref.shape
    pad_ref[...] = jnp.zeros(pad_ref.shape, f32)
    row_ref[...] = jnp.zeros(row_ref.shape, i32)
    row_ref[0:directions, 0:capacity] = sent_ref[...]
    head = 3 * own_blocks
    list_rows = list_ref.shape[1] - 4
    for s, ref in enumerate(given):
        slot = ref[head : head + 2 * list_rows].astype(i32)
        block = jnp.full(slot.shape, block_total, i32)
        for k in range(directions):
            here = (slot >= k * capacity) & (slot < (k + 1) * capacity)
            row = jnp.broadcast_to(row_ref[k : k + 1, :], slot.shape)
            at = jnp.where(here, slot - k * capacity, 0)
            block = jnp.where(here, jnp.take_along_axis(row, at, axis=1), block)
        rest = ref[head + 2 * list_rows :].astype(i32)
        codes = coded(rest[0:list_rows], block[0:list_rows], block[list_rows:])
        finished_list(list_ref.at[s], codes, block_total, rest[list_rows:])
    list_ref[len(given)] = own_ref[...]
    sent = pltpu.make_async_copy(list_ref, smem_ref, arrival)
    sent.start()
    target_ref[len(given) * own_blocks :] = near_ref[...]
    for s, ref in enumerate(given):

        def some_targets(n, _):
            for q in range(slots):
                t = n * slots + q
                for r in range(3):
                    row = ref[pl.ds(r * own_blocks + t, 1), :]
                    pad_ref[q, r : r + 1, :] = (row - centre_km) * scale
                offsets = pad_ref[q]
                norm = -0.5 * jnp.sum(offsets * offsets, axis=0, keepdims=True)
                target_ref[s * own_blocks + t] = target_features(offsets, norm)
            return 0

        lax.fori_loop(0, own_blocks // slots, some_targets, 0)
    sent.wait()


def halo_features(own_list, targets, sent, given, block_total):
    own_blocks = targets.shape[0]
    list_rows = (given[0].shape[0] - 3 * own_blocks) // 4
    lists = (len(given) + 1, list_rows + 4, BLOCK)
    return pl.pallas_call(
        functools.partial(halo_features_kernel, block_total, own_blocks),
        out_shape=(
            pltpu.VMEM(((len(given) + 1) * own_blocks, FEATURES, BLOCK), bf16),
            pltpu.SMEM(lists, i32),
        ),
        in_specs=[vmem()] * (len(given) + 3),
        out_specs=(vmem(), smem()),
        scratch_shapes=[
            pltpu.VMEM(lists, i32),
            pltpu.VMEM((SLOTS, 8, BLOCK), f32),
            pltpu.VMEM((8, BLOCK), i32),
            pltpu.SemaphoreType.DMA,
        ],
        compiler_params=params(8),
        cost_estimate=lasting(1),
        name="halo_features",
    )(*held(own_list, targets), sent, *given)


def value_rows(first, second):
    row = lax.broadcasted_iota(i32, (8, BLOCK), 0)
    both = jnp.where((row & 1) == 1, first, second)
    high, middle, low = split(both)
    rows = jnp.where(row < 5, jnp.where(row < 3, high, middle), jnp.where(row < 7, low, 0.0))
    rows = jnp.where(row == 0, 1.0, rows).astype(bf16)
    return jnp.concatenate([rows, rows], axis=1)


def half_kernel(event_ref, mine_ref, near_ref, *refs):
    parcels, (out_ref, *sent) = refs[: len(refs) // 2], refs[len(refs) // 2 :]
    half = out_ref.shape[1]
    at = pl.ds(pl.multiple_of((event_ref[0] & 1) * half, half), half)
    out_ref[...] = mine_ref[...] + near_ref[:, at]
    for given, to in zip(parcels, sent):
        to[...] = given[...]


def half_sum(event, mine, near, parcels):
    return pl.pallas_call(
        half_kernel,
        out_shape=[jax.ShapeDtypeStruct(a.shape, f32) for a in (mine, *parcels)],
        in_specs=[smem()] + [vmem()] * (len(parcels) + 2),
        out_specs=[vmem()] * (len(parcels) + 1),
        compiler_params=params(4),
        cost_estimate=lasting(0.1),
        name="half_sum",
    )(event, *held(mine), near, *parcels)


def add_kernel(first_ref, second_ref, mark_ref, out_ref):
    out_ref[...] = first_ref[...] + second_ref[...]


def added(first, second, mark):
    return pl.pallas_call(
        add_kernel,
        out_shape=jax.ShapeDtypeStruct(first.shape, f32),
        in_specs=[vmem()] * 3,
        out_specs=vmem(),
        compiler_params=params(4),
        cost_estimate=lasting(0.1),
        name="added",
    )(first, second, mark)


def schedule(list_ref):
    sets, list_rows = list_ref.shape[0], list_ref.shape[1] - 4
    ends = []
    for s in range(sets):
        ends.append(list_ref[s, list_rows + 1, 0] + (ends[-1] if ends else 0))
    halo_steps, all_steps = [(e + STEP - 1) >> STEP_BITS for e in ends[-2:]]
    return ends, jnp.maximum(halo_steps, jnp.minimum(QUOTA, all_steps)), all_steps


class Totals:
    def __init__(self, ends, own_blocks, first_set, refs):
        self.ends, self.own_blocks, self.first_set = ends, own_blocks, first_set
        self.lists, self.sources, self.targets, self.values = refs[:4]
        self.exponent_ref, self.weight_ref, self.sum_ref = refs[4:]

    def chunk(self, i):
        s, base = 0, 0
        for end in self.ends[:-1]:
            past = i >= end
            s = s + past.astype(i32)
            base = jnp.where(past, end, base)
        at = i - base
        t, first, second = decoded(self.lists[s, at >> 7, at & (BLOCK - 1)])
        return s * self.own_blocks + t, first, second

    def exponents(self, k, c):
        t, first, second = self.chunk(k * STEP + c)
        both = jnp.concatenate([self.sources[first], self.sources[second]], axis=0)
        exponent = jnp.dot(both, self.targets[t], preferred_element_type=f32)
        self.exponent_ref[c, :, 0:BLOCK] = exponent[0:BLOCK]
        self.exponent_ref[c, :, BLOCK:] = exponent[BLOCK:]

    def weights(self, c):
        weight = jnp.exp2(self.exponent_ref[c])
        high = weight.astype(bf16)
        self.weight_ref[c, 0:BLOCK] = high
        self.weight_ref[c, BLOCK : 2 * BLOCK] = (weight - high.astype(f32)).astype(bf16)

    def sums(self, k, c):
        t, first, second = self.chunk(k * STEP + c)
        values = jnp.concatenate([self.values[first], self.values[second]], axis=0)
        both = jnp.dot(values, self.weight_ref[c], preferred_element_type=f32)
        at = pl.ds(pl.multiple_of((t - self.first_set * self.own_blocks) * 8, 8), 8)
        self.sum_ref[at, :] += both[0:8, 0:BLOCK] + both[8:16, BLOCK : 2 * BLOCK]

    def steps(self, begin, end):
        def step(k, _):
            for c in range(STEP):
                self.weights(c)
                self.sums(k, c)
                self.exponents(k + 1, c)
            return 0

        lax.fori_loop(begin, end, step, 0)

    def finish(self, s, out_ref):
        rows = [
            self.sum_ref[pl.ds(s * self.own_blocks * 8 + r, self.own_blocks, stride=8), :]
            for r in range(7)
        ]
        out_ref[0] = rows[0]
        out_ref[1] = rows[1] + rows[3] + rows[5]
        out_ref[2] = rows[2] + rows[4] + rows[6]


def first_totals_kernel(own_blocks, list_ref, source_ref, target_ref, *refs):
    *refs, sum_ref, weight_ref = refs
    sets = list_ref.shape[0]
    own_sum_ref, value_ref, exponent_ref = refs[-3:]
    out_refs = refs[-3 - (sets - 1) : -3]
    summed = refs[: -3 - (sets - 1)]
    ends, first_steps, _ = schedule(list_ref)
    given = [list_ref, source_ref, target_ref, value_ref, exponent_ref, weight_ref, sum_ref]
    totals = Totals(ends, own_blocks, 0, given)
    sum_ref[...] = jnp.zeros(sum_ref.shape, f32)
    block_total = value_ref.shape[0] - 1
    rounds = 1

    def begin(n, _):
        for c in range(STEP // rounds):
            totals.exponents(0, n * (STEP // rounds) + c)
        for c in range(block_total // rounds):
            b = n * (block_total // rounds) + c
            at = pl.ds(pl.multiple_of(b * BLOCK, BLOCK), BLOCK)
            both = sum(ref[:, at] for ref in summed)
            value_ref[b] = value_rows(both[0:1], both[1:2])
        return 0

    if len(summed) == 1:
        lax.fori_loop(0, rounds, begin, 0)
    else:
        begin_from_halves(totals, summed, value_ref, rounds)
    value_ref[block_total] = jnp.zeros((8, 2 * BLOCK), bf16)
    totals.steps(0, first_steps)
    for s in range(sets - 1):
        totals.finish(s, out_refs[s])
    own_sum_ref[...] = sum_ref[(sets - 1) * own_blocks * 8 :, :]


def begin_from_halves(totals, summed, value_ref, rounds):
    event_ref, *halves = summed
    half_blocks = (value_ref.shape[0] - 1) // 2
    core = event_ref[0] & 1

    def begin(n, _):
        for c in range(STEP // rounds):
            totals.exponents(0, n * (STEP // rounds) + c)
        for piece, ref in enumerate(halves):
            for c in range(half_blocks // rounds):
                b = n * (half_blocks // rounds) + c
                at = pl.ds(pl.multiple_of(b * BLOCK, BLOCK), BLOCK)
                where = (core ^ piece) * half_blocks + b
                totals.values[where] = value_rows(ref[0:1, at], ref[1:2, at])
        return 0

    lax.fori_loop(0, rounds, begin, 0)


def first_totals(lists, sources, targets, summed, block_total):
    sets = lists.shape[0]
    own_blocks = targets.shape[0] // sets
    specs = [smem()] * (len(summed) - 2) + [vmem()] * min(len(summed), 2)
    return pl.pallas_call(
        functools.partial(first_totals_kernel, own_blocks),
        out_shape=[jax.ShapeDtypeStruct((3, own_blocks, BLOCK), f32)] * (sets - 1)
        + [
            pltpu.VMEM((own_blocks * 8, BLOCK), f32),
            pltpu.VMEM((block_total + 1, 8, 2 * BLOCK), bf16),
            pltpu.VMEM((STEP, BLOCK, 2 * BLOCK), f32),
        ],
        in_specs=[smem(), vmem(), vmem()] + specs,
        out_specs=[vmem()] * (sets + 2),
        scratch_shapes=[
            pltpu.VMEM((sets * own_blocks * 8, BLOCK), f32),
            pltpu.VMEM((STEP, 2 * BLOCK, 2 * BLOCK), bf16),
        ],
        compiler_params=params(14),
        cost_estimate=lasting(8),
        name="first_totals",
    )(pltpu.with_memory_space_constraint(lists, pltpu.SMEM), *held(sources, targets), *summed)


def last_totals_kernel(
    own_blocks, list_ref, source_ref, target_ref, value_ref, own_sum_ref, _, out_ref,
    exponent_ref, sum_ref, weight_ref,
):
    ends, first_steps, all_steps = schedule(list_ref)
    given = [list_ref, source_ref, target_ref, value_ref, exponent_ref, weight_ref, sum_ref]
    totals = Totals(ends, own_blocks, list_ref.shape[0] - 1, given)
    sum_ref[...] = own_sum_ref[...]
    totals.steps(first_steps, all_steps)
    totals.finish(0, out_ref)


def last_totals(lists, sources, targets, values, own_sum, exponent):
    own_blocks = targets.shape[0] // lists.shape[0]
    lists = pltpu.with_memory_space_constraint(lists, pltpu.SMEM)
    total, _ = pl.pallas_call(
        functools.partial(last_totals_kernel, own_blocks),
        out_shape=[
            jax.ShapeDtypeStruct((3, own_blocks, BLOCK), f32),
            pltpu.VMEM(exponent.shape, f32),
        ],
        in_specs=[smem()] + [vmem()] * 5,
        out_specs=[vmem()] * 2,
        scratch_shapes=[
            pltpu.VMEM((own_blocks * 8, BLOCK), f32),
            pltpu.VMEM((STEP, 2 * BLOCK, 2 * BLOCK), bf16),
        ],
        input_output_aliases={5: 1},
        compiler_params=params(14),
        cost_estimate=lasting(8),
        name="last_totals",
    )(lists, *held(sources, targets, values, own_sum, exponent))
    return total


def smoothed_kernel(*refs):
    *parts, out_ref = refs
    totals = [sum(part[r] for part in parts) for r in range(3)]
    for k in range(2):
        ratio = totals[k + 1] / totals[0]
        for t in range(ratio.shape[0]):
            out_ref[k : k + 1, t * BLOCK : (t + 1) * BLOCK] = ratio[t : t + 1]


def smoothed(parts):
    return pl.pallas_call(
        smoothed_kernel,
        out_shape=jax.ShapeDtypeStruct((2, parts[0].shape[1] * BLOCK), f32),
        in_specs=[vmem()] * len(parts),
        out_specs=vmem(),
        compiler_params=params(4),
        cost_estimate=lasting(0.2),
        name="smoothed",
    )(*parts)


def local(partials, coords, volume, send_blocks, halo_counts, source_slots, source_counts):
    cut_count = lax.axis_size("cuts")
    event_count = lax.axis_size("event")
    block_total = volume.shape[0] // BLOCK
    own_blocks = source_slots.shape[2]
    grid_step = cut_count // 4
    my_event = lax.axis_index("event")

    strides = [(1, [[0], [1]])]
    if grid_step == 1:
        strides = [(1, [[0, 2], [1, 3]])]
    else:
        strides.append((grid_step, [[2], [3]]))
    event = my_event.reshape(1)
    mine = partials[0]
    near_coords, near_volume, near_mine, own_list, *parcels = prepare(
        strides, send_blocks.shape[3], event, lax.axis_index("cuts").reshape(1), halo_counts[0],
        source_slots[0, 0].T, source_counts[0], coords, volume.reshape(block_total, BLOCK),
        mine,
    )
    turns = [(stride, turn) for stride, _ in strides for turn in (1, 0)]
    if event_count == 4:
        part, *parcels = half_sum(event, near_mine, crossed(mine, "event", 1), parcels)
        far_part = crossed(part, "event", 2)
    arrived = [swapped(p, *turn) for p, turn in zip(parcels, turns)]
    sources, targets, mark = own_features(event, near_coords, near_volume, own_blocks)
    if event_count == 4:
        part = added(part, far_part, mark)
        summed = [event, part, crossed(part, "event", 1)]
    else:
        summed = [lax.psum(mine, "event")]

    targets, lists = halo_features(
        own_list, targets, send_blocks[0, 0], arrived, block_total
    )
    *halo_totals, own_sum, values, exponent = first_totals(
        lists, sources, targets, summed, block_total
    )
    returned = [swapped(t, *turn) for t, turn in zip(halo_totals, turns)]
    totals = last_totals(lists, sources, targets, values, own_sum, exponent)
    return smoothed([totals, *returned])


def solution(mesh):
    placed = (
        P("event", None, ("runs", "cuts")),
        P(None, ("runs", "cuts")),
        P(("runs", "cuts")),
        P(("runs", "cuts"), "event", None, None),
        P(("runs", "cuts"), "event", None),
        P(("runs", "cuts"), "event", None, None),
        P(("runs", "cuts"), "event", None),
    )
    return jax.shard_map(
        local,
        mesh=mesh,
        in_specs=placed,
        out_specs=P(None, ("runs", "cuts", "event")),
        check_vma=False,
    )
```

```python
import functools
import math

import jax
import jax.numpy as jnp
from jax import lax
from jax.experimental import pallas as pl
from jax.experimental.pallas import tpu as pltpu
from jax.sharding import PartitionSpec as P

BLOCK = 128
FEATURES = 48
STEP_BITS = 5
STEP = 1 << STEP_BITS
SLOTS = 32
QUOTA = 4
FIELD = 10
sigma_km = 50.0
centre_km = 400.0
scale = math.sqrt(math.log2(math.e)) / sigma_km

f32 = jnp.float32
bf16 = jnp.bfloat16
i32 = jnp.int32


def vmem():
    return pl.BlockSpec(memory_space=pltpu.VMEM)


def smem():
    return pl.BlockSpec(memory_space=pltpu.SMEM)


def held(*arrays):
    return [pltpu.with_memory_space_constraint(a, pltpu.VMEM) for a in arrays]


def far(*arrays):
    return [pltpu.with_memory_space_constraint(a, pltpu.HBM) for a in arrays]


def lasting(microseconds):
    flops = int(microseconds * 1.15e9)
    return pl.CostEstimate(flops=flops, bytes_accessed=1000000, transcendentals=0)


def params(mib):
    return pltpu.CompilerParams(vmem_limit_bytes=mib << 20)


def swapped(block, stride, turn):
    devices = lax.axis_size("cuts")
    step = [stride, -stride] if turn == 0 else [-stride, stride]
    route = [(i, (i + step[(i // stride) % 2]) % devices) for i in range(devices)]
    return lax.ppermute(block, "cuts", route)


def crossed(block, axis, bit):
    route = [(i ^ bit, i) for i in range(lax.axis_size(axis))]
    return lax.ppermute(block, axis, route)


def split(values):
    high = values.astype(bf16).astype(f32)
    rest = values - high
    middle = rest.astype(bf16).astype(f32)
    return high, middle, rest - middle


def feature_rows(offsets, fourth, fifth):
    row = lax.broadcasted_iota(i32, (8, BLOCK), 0)
    rows = jnp.where(row == 3, fourth, jnp.where(row == 4, fifth, 0.0))
    return jnp.where(row < 3, offsets, rows)


def place(coords_ref, b):
    at = pl.ds(pl.multiple_of(b * BLOCK, BLOCK), BLOCK)
    offsets = (coords_ref[:, at] - centre_km) * scale
    squares = offsets * offsets
    norm = -0.5 * (squares[0:1] + squares[1:2] + squares[2:3])
    return jnp.concatenate([offsets, jnp.zeros((5, BLOCK), f32)], axis=0), norm


def target_features(offsets, norm):
    high, middle, low = split(feature_rows(offsets, 1.0, norm))
    return jnp.concatenate([high, middle, low, high, middle, high], axis=0).astype(bf16)


def own_features_kernel(
    event_ref, coords_ref, volume_ref, source_ref, target_ref, mark_ref, log_ref
):
    block_total = volume_ref.shape[0]
    own_blocks = target_ref.shape[0]
    slots = SLOTS
    log_ref[...] = jnp.log2(volume_ref[...])

    def some_sources(n, _):
        for slot in range(slots):
            b = n * slots + slot
            offsets, norm = place(coords_ref, b)
            high, middle, low = split(feature_rows(offsets, norm + log_ref[pl.ds(b, 1), :], 1.0))
            rows = jnp.concatenate([high, high, high, middle, middle, low], axis=0)
            source_ref[b] = rows.astype(bf16).T
        return 0

    def some_targets(n, _):
        for slot in range(slots):
            t = n * slots + slot
            block = event_ref[0] * own_blocks + t
            target_ref[t] = target_features(*place(coords_ref, block))
        return 0

    lax.fori_loop(0, block_total // slots, some_sources, 0)
    lax.fori_loop(0, own_blocks // slots, some_targets, 0)
    column = lax.broadcasted_iota(i32, (BLOCK, FEATURES), 1)
    source_ref[block_total] = jnp.where(column == 3, -10000.0, 0.0).astype(bf16)
    mark_ref[...] = jnp.zeros(mark_ref.shape, f32)


def own_features(event, coords, volume, own_blocks):
    block_total = volume.shape[0]
    return pl.pallas_call(
        own_features_kernel,
        out_shape=(
            pltpu.VMEM((block_total + 1, BLOCK, FEATURES), bf16),
            pltpu.VMEM((own_blocks, FEATURES, BLOCK), bf16),
            jax.ShapeDtypeStruct((8, BLOCK), f32),
        ),
        in_specs=[smem(), vmem(), vmem()],
        out_specs=(vmem(),) * 3,
        scratch_shapes=[pltpu.VMEM((block_total, BLOCK), f32)],
        compiler_params=params(8),
        cost_estimate=lasting(4),
        name="own_features",
    )(event, *held(coords, volume))


def coded(target, first, second):
    return (target << (2 * FIELD)) + (second << FIELD) + first


def finished_list(ref, codes, spare, count):
    list_rows = codes.shape[0]
    ref[0:list_rows] = codes
    ref[list_rows : list_rows + 1] = jnp.full((1, BLOCK), coded(0, spare, spare), i32)
    ref[list_rows + 1 :] = count[0:3]


def decoded(code):
    mask = (1 << FIELD) - 1
    return code >> (2 * FIELD), code & mask, (code >> FIELD) & mask


def prepare_kernel(
    strides, capacity, event_ref, cut_ref, halo_given, slot_given, count_given, coords_given,
    volume_given, mine_given, coords_ref, volume_ref, mine_ref, own_ref, *refs,
):
    parcels, rest = refs[: 2 * len(strides)], refs[2 * len(strides) :]
    halo_ref, slot_ref, count_ref, row_ref, arrival = rest
    width, own_blocks = slot_ref.shape
    block_total = volume_ref.shape[0]
    sets = len(parcels) + 1
    brought = [
        (halo_given, halo_ref), (slot_given, slot_ref), (count_given, count_ref),
        (coords_given, coords_ref), (volume_given, volume_ref), (mine_given, mine_ref),
    ]
    half = mine_ref.shape[1]
    at = pl.ds(pl.multiple_of((event_ref[0] & 1) * half, half), half)
    brought[5] = (mine_given.at[:, at], mine_ref)
    brought = [
        pltpu.make_async_copy(given, ref, arrival.at[n]) for n, (given, ref) in enumerate(brought)
    ]
    for copy in brought:
        copy.start()
    for copy in brought[:3]:
        copy.wait()
    row_ref[...] = jnp.zeros(row_ref.shape, i32)
    row_ref[0:width, 0:own_blocks] = slot_ref[...]
    row_ref[width : width + 1, 0:own_blocks] = count_ref[...]
    shape = (width, BLOCK)
    slots = row_ref[0:width]
    used = lax.broadcasted_iota(i32, shape, 0) < row_ref[width : width + 1]
    halo = slots - block_total
    lives = [used & (halo < 0)]
    for stride, members in strides:
        both = []
        for directions in members:
            live = jnp.zeros(shape, i32)
            for k in directions:
                near = (halo >= k * capacity) & (halo - k * capacity < halo_ref[0, k])
                live = live + (near & (halo < (k + 1) * capacity)).astype(i32)
            both.append(live)
        odd = (cut_ref[0] // stride) % 2
        for first, second in (both, both[::-1]):
            live = first * (1 - odd) + second * odd
            lives.append(used & (live > 0))
    rows = sets * width
    live = jnp.concatenate([l.astype(f32) for l in lives], axis=0).astype(bf16)
    near = lax.broadcasted_iota(i32, (rows, rows), 0)
    across = lax.broadcasted_iota(i32, (rows, rows), 1)
    alike = near // width == across // width
    above = (alike & (across < near)).astype(f32).astype(bf16)
    rank = jnp.dot(above, live, preferred_element_type=f32).astype(i32)
    count = jnp.dot(alike.astype(f32).astype(bf16), live, preferred_element_type=f32)
    twos = ((count.astype(i32) + 1) >> 1).astype(f32).astype(bf16)
    near = lax.broadcasted_iota(i32, (BLOCK, BLOCK), 0)
    across = lax.broadcasted_iota(i32, (BLOCK, BLOCK), 1)
    earlier = (near < across).astype(f32).astype(bf16)
    before = jnp.dot(twos, earlier, preferred_element_type=f32).astype(i32)
    total = jnp.dot(twos, jnp.ones((BLOCK, BLOCK), bf16), preferred_element_type=f32).astype(i32)
    place_of = before + (rank >> 1)
    list_rows = own_blocks * width // (2 * BLOCK)
    high = jnp.full(shape, -1, i32)
    low = jnp.zeros(shape, i32)
    odd = jnp.zeros(shape, i32)
    for s in range(sets):
        part = slice(s * width, (s + 1) * width)
        high = jnp.where(lives[s], (place_of[part] >> 7) + s * list_rows, high)
        low = jnp.where(lives[s], place_of[part] & (BLOCK - 1), low)
        odd = jnp.where(lives[s], rank[part] & 1, odd)
    block = jnp.where(halo < 0, slots, halo) + 1
    even = 1 - odd
    target = lax.broadcasted_iota(i32, shape, 1)
    parts = [target * even, (block >> 3) * even, (block & 7) * even]
    parts = [p.astype(f32) for p in parts + [(block >> 3) * odd, (block & 7) * odd]]
    size = (sets * list_rows + 7) // 8 * 8
    list_row = lax.broadcasted_iota(i32, (size, BLOCK), 0)
    list_lane = lax.broadcasted_iota(i32, (BLOCK, BLOCK), 0)
    codes, places = [], []
    for i in range(width):
        hit = list_row == high[i : i + 1, :]
        codes.append(
            jnp.concatenate([jnp.where(hit, p[i : i + 1, :], 0.0) for p in parts], axis=0)
        )
        places.append((list_lane == low[i : i + 1, :]).astype(f32).astype(bf16))
    codes = jnp.concatenate([c.astype(bf16) for c in codes], axis=1)
    places = jnp.concatenate(places, axis=1)
    found = lax.dot_general(
        codes, places, (((1,), (1,)), ((), ())), preferred_element_type=f32
    ).astype(i32)
    target, *found = [found[n * size : (n + 1) * size] for n in range(5)]
    blocks = [found[0] * 8 + found[1] - 1, found[2] * 8 + found[3] - 1]
    for s in range(sets):
        part = slice(s * list_rows, (s + 1) * list_rows)
        spare = block_total if s == 0 else 4 * capacity
        pair = [jnp.where(b[part] < 0, spare, b[part]) for b in blocks]
        count = total[s * width : s * width + list_rows]
        if s == 0:
            finished_list(own_ref, coded(target[part], *pair), spare, count)
        else:
            given = [*pair, target[part], count]
            for n, values in enumerate(given):
                at = 3 * own_blocks + n * list_rows
                parcels[s - 1][at : at + list_rows] = values.astype(f32)
    for copy in brought[3:]:
        copy.wait()

    def some_coords(t, _):
        at = pl.multiple_of((event_ref[0] * own_blocks + t) * BLOCK, BLOCK)
        given = coords_ref[:, pl.ds(at, BLOCK)]
        for parcel in parcels:
            for r in range(3):
                parcel[pl.ds(r * own_blocks + t, 1), :] = given[r : r + 1]
        return 0

    lax.fori_loop(0, own_blocks, some_coords, 0, unroll=8)


def prepare(strides, capacity, event, cut, halo_counts, slots, counts, coords, volume, mine):
    width, own_blocks = slots.shape
    list_rows = own_blocks * width // (2 * BLOCK)
    parcel = jax.ShapeDtypeStruct((3 * own_blocks + 4 * list_rows, BLOCK), f32)
    return pl.pallas_call(
        functools.partial(prepare_kernel, strides, capacity),
        out_shape=(
            pltpu.VMEM(coords.shape, f32),
            pltpu.VMEM(volume.shape, f32),
            pltpu.VMEM((2, mine.shape[1] // 2), f32),
            pltpu.VMEM((list_rows + 4, BLOCK), i32),
        )
        + (parcel,) * (2 * len(strides)),
        in_specs=[smem()] * 2 + [pl.BlockSpec(memory_space=pltpu.HBM)] * 6,
        out_specs=(vmem(),) * 4 + (vmem(),) * (2 * len(strides)),
        scratch_shapes=[
            pltpu.SMEM(halo_counts.shape, i32),
            pltpu.VMEM(slots.shape, i32),
            pltpu.VMEM(counts.shape, i32),
            pltpu.VMEM((width + 8, BLOCK), i32),
            pltpu.SemaphoreType.DMA((6,)),
        ],
        compiler_params=params(8),
        cost_estimate=lasting(2),
        name="prepare",
    )(event, cut, *far(halo_counts, slots, counts, coords, volume, mine))


def halo_features_kernel(block_total, own_blocks, own_ref, near_ref, sent_ref, *refs):
    *given, target_ref, smem_ref, list_ref, pad_ref, row_ref, arrival = refs
    slots = pad_ref.shape[0]
    directions, capacity = sent_ref.shape
    pad_ref[...] = jnp.zeros(pad_ref.shape, f32)
    row_ref[...] = jnp.zeros(row_ref.shape, i32)
    row_ref[0:directions, 0:capacity] = sent_ref[...]
    head = 3 * own_blocks
    list_rows = list_ref.shape[1] - 4
    for s, ref in enumerate(given):
        slot = ref[head : head + 2 * list_rows].astype(i32)
        block = jnp.full(slot.shape, block_total, i32)
        for k in range(directions):
            here = (slot >= k * capacity) & (slot < (k + 1) * capacity)
            row = jnp.broadcast_to(row_ref[k : k + 1, :], slot.shape)
            at = jnp.where(here, slot - k * capacity, 0)
            block = jnp.where(here, jnp.take_along_axis(row, at, axis=1), block)
        rest = ref[head + 2 * list_rows :].astype(i32)
        codes = coded(rest[0:list_rows], block[0:list_rows], block[list_rows:])
        finished_list(list_ref.at[s], codes, block_total, rest[list_rows:])
    list_ref[len(given)] = own_ref[...]
    sent = pltpu.make_async_copy(list_ref, smem_ref, arrival)
    sent.start()
    target_ref[len(given) * own_blocks :] = near_ref[...]
    for s, ref in enumerate(given):

        def some_targets(n, _):
            for q in range(slots):
                t = n * slots + q
                for r in range(3):
                    row = ref[pl.ds(r * own_blocks + t, 1), :]
                    pad_ref[q, r : r + 1, :] = (row - centre_km) * scale
                offsets = pad_ref[q]
                norm = -0.5 * jnp.sum(offsets * offsets, axis=0, keepdims=True)
                target_ref[s * own_blocks + t] = target_features(offsets, norm)
            return 0

        lax.fori_loop(0, own_blocks // slots, some_targets, 0)
    sent.wait()


def halo_features(own_list, targets, sent, given, block_total):
    own_blocks = targets.shape[0]
    list_rows = (given[0].shape[0] - 3 * own_blocks) // 4
    lists = (len(given) + 1, list_rows + 4, BLOCK)
    return pl.pallas_call(
        functools.partial(halo_features_kernel, block_total, own_blocks),
        out_shape=(
            pltpu.VMEM(((len(given) + 1) * own_blocks, FEATURES, BLOCK), bf16),
            pltpu.SMEM(lists, i32),
        ),
        in_specs=[vmem()] * (len(given) + 3),
        out_specs=(vmem(), smem()),
        scratch_shapes=[
            pltpu.VMEM(lists, i32),
            pltpu.VMEM((SLOTS, 8, BLOCK), f32),
            pltpu.VMEM((8, BLOCK), i32),
            pltpu.SemaphoreType.DMA,
        ],
        compiler_params=params(8),
        cost_estimate=lasting(1),
        name="halo_features",
    )(*held(own_list, targets), sent, *given)


def value_rows(first, second):
    row = lax.broadcasted_iota(i32, (8, BLOCK), 0)
    both = jnp.where((row & 1) == 1, first, second)
    high, middle, low = split(both)
    rows = jnp.where(row < 5, jnp.where(row < 3, high, middle), jnp.where(row < 7, low, 0.0))
    rows = jnp.where(row == 0, 1.0, rows).astype(bf16)
    return jnp.concatenate([rows, rows], axis=1)


def half_kernel(event_ref, mine_ref, near_ref, *refs):
    parcels, (out_ref, *sent) = refs[: len(refs) // 2], refs[len(refs) // 2 :]
    half = out_ref.shape[1]
    at = pl.ds(pl.multiple_of((event_ref[0] & 1) * half, half), half)
    out_ref[...] = mine_ref[...] + near_ref[:, at]
    for given, to in zip(parcels, sent):
        to[...] = given[...]


def half_sum(event, mine, near, parcels):
    return pl.pallas_call(
        half_kernel,
        out_shape=[jax.ShapeDtypeStruct(a.shape, f32) for a in (mine, *parcels)],
        in_specs=[smem()] + [vmem()] * (len(parcels) + 2),
        out_specs=[vmem()] * (len(parcels) + 1),
        compiler_params=params(4),
        cost_estimate=lasting(0.1),
        name="half_sum",
    )(event, *held(mine), near, *parcels)


def add_kernel(first_ref, second_ref, mark_ref, out_ref):
    out_ref[...] = first_ref[...] + second_ref[...]


def added(first, second, mark):
    return pl.pallas_call(
        add_kernel,
        out_shape=jax.ShapeDtypeStruct(first.shape, f32),
        in_specs=[vmem()] * 3,
        out_specs=vmem(),
        compiler_params=params(4),
        cost_estimate=lasting(0.1),
        name="added",
    )(first, second, mark)


def schedule(list_ref):
    sets, list_rows = list_ref.shape[0], list_ref.shape[1] - 4
    ends = []
    for s in range(sets):
        ends.append(list_ref[s, list_rows + 1, 0] + (ends[-1] if ends else 0))
    halo_steps, all_steps = [(e + STEP - 1) >> STEP_BITS for e in ends[-2:]]
    return ends, jnp.maximum(halo_steps, jnp.minimum(QUOTA, all_steps)), all_steps


class Totals:
    def __init__(self, ends, own_blocks, first_set, refs):
        self.ends, self.own_blocks, self.first_set = ends, own_blocks, first_set
        self.lists, self.sources, self.targets, self.values = refs[:4]
        self.exponent_ref, self.weight_ref, self.sum_ref = refs[4:]

    def chunk(self, i):
        s, base = 0, 0
        for end in self.ends[:-1]:
            past = i >= end
            s = s + past.astype(i32)
            base = jnp.where(past, end, base)
        at = i - base
        t, first, second = decoded(self.lists[s, at >> 7, at & (BLOCK - 1)])
        return s * self.own_blocks + t, first, second

    def exponents(self, k, c):
        t, first, second = self.chunk(k * STEP + c)
        both = jnp.concatenate([self.sources[first], self.sources[second]], axis=0)
        exponent = jnp.dot(both, self.targets[t], preferred_element_type=f32)
        self.exponent_ref[c, :, 0:BLOCK] = exponent[0:BLOCK]
        self.exponent_ref[c, :, BLOCK:] = exponent[BLOCK:]

    def weights(self, c):
        weight = jnp.exp2(self.exponent_ref[c])
        high = weight.astype(bf16)
        self.weight_ref[c, 0:BLOCK] = high
        self.weight_ref[c, BLOCK : 2 * BLOCK] = (weight - high.astype(f32)).astype(bf16)

    def sums(self, k, c):
        t, first, second = self.chunk(k * STEP + c)
        values = jnp.concatenate([self.values[first], self.values[second]], axis=0)
        both = jnp.dot(values, self.weight_ref[c], preferred_element_type=f32)
        at = pl.ds(pl.multiple_of((t - self.first_set * self.own_blocks) * 8, 8), 8)
        self.sum_ref[at, :] += both[0:8, 0:BLOCK] + both[8:16, BLOCK : 2 * BLOCK]

    def steps(self, begin, end):
        def step(k, _):
            for c in range(STEP):
                self.weights(c)
                self.sums(k, c)
                self.exponents(k + 1, c)
            return 0

        lax.fori_loop(begin, end, step, 0)

    def finish(self, s, out_ref):
        rows = [
            self.sum_ref[pl.ds(s * self.own_blocks * 8 + r, self.own_blocks, stride=8), :]
            for r in range(7)
        ]
        out_ref[0] = rows[0]
        out_ref[1] = rows[1] + rows[3] + rows[5]
        out_ref[2] = rows[2] + rows[4] + rows[6]


def first_totals_kernel(own_blocks, list_ref, source_ref, target_ref, *refs):
    *refs, sum_ref, weight_ref = refs
    sets = list_ref.shape[0]
    own_sum_ref, value_ref, exponent_ref = refs[-3:]
    out_refs = refs[-3 - (sets - 1) : -3]
    summed = refs[: -3 - (sets - 1)]
    ends, first_steps, _ = schedule(list_ref)
    given = [list_ref, source_ref, target_ref, value_ref, exponent_ref, weight_ref, sum_ref]
    totals = Totals(ends, own_blocks, 0, given)
    sum_ref[...] = jnp.zeros(sum_ref.shape, f32)
    block_total = value_ref.shape[0] - 1
    rounds = 1

    def begin(n, _):
        for c in range(STEP // rounds):
            totals.exponents(0, n * (STEP // rounds) + c)
        for c in range(block_total // rounds):
            b = n * (block_total // rounds) + c
            at = pl.ds(pl.multiple_of(b * BLOCK, BLOCK), BLOCK)
            both = sum(ref[:, at] for ref in summed)
            value_ref[b] = value_rows(both[0:1], both[1:2])
        return 0

    if len(summed) == 1:
        lax.fori_loop(0, rounds, begin, 0)
    else:
        begin_from_halves(totals, summed, value_ref, rounds)
    value_ref[block_total] = jnp.zeros((8, 2 * BLOCK), bf16)
    totals.steps(0, first_steps)
    for s in range(sets - 1):
        totals.finish(s, out_refs[s])
    own_sum_ref[...] = sum_ref[(sets - 1) * own_blocks * 8 :, :]


def begin_from_halves(totals, summed, value_ref, rounds):
    event_ref, *halves = summed
    half_blocks = (value_ref.shape[0] - 1) // 2
    core = event_ref[0] & 1

    def begin(n, _):
        for c in range(STEP // rounds):
            totals.exponents(0, n * (STEP // rounds) + c)
        for piece, ref in enumerate(halves):
            for c in range(half_blocks // rounds):
                b = n * (half_blocks // rounds) + c
                at = pl.ds(pl.multiple_of(b * BLOCK, BLOCK), BLOCK)
                where = (core ^ piece) * half_blocks + b
                totals.values[where] = value_rows(ref[0:1, at], ref[1:2, at])
        return 0

    lax.fori_loop(0, rounds, begin, 0)


def first_totals(lists, sources, targets, summed, block_total):
    sets = lists.shape[0]
    own_blocks = targets.shape[0] // sets
    specs = [smem()] * (len(summed) - 2) + [vmem()] * min(len(summed), 2)
    return pl.pallas_call(
        functools.partial(first_totals_kernel, own_blocks),
        out_shape=[jax.ShapeDtypeStruct((3, own_blocks, BLOCK), f32)] * (sets - 1)
        + [
            pltpu.VMEM((own_blocks * 8, BLOCK), f32),
            pltpu.VMEM((block_total + 1, 8, 2 * BLOCK), bf16),
            pltpu.VMEM((STEP, BLOCK, 2 * BLOCK), f32),
        ],
        in_specs=[smem(), vmem(), vmem()] + specs,
        out_specs=[vmem()] * (sets + 2),
        scratch_shapes=[
            pltpu.VMEM((sets * own_blocks * 8, BLOCK), f32),
            pltpu.VMEM((STEP, 2 * BLOCK, 2 * BLOCK), bf16),
        ],
        compiler_params=params(14),
        cost_estimate=lasting(8),
        name="first_totals",
    )(pltpu.with_memory_space_constraint(lists, pltpu.SMEM), *held(sources, targets), *summed)


def last_totals_kernel(
    own_blocks, list_ref, source_ref, target_ref, value_ref, own_sum_ref, _, out_ref,
    exponent_ref, sum_ref, weight_ref,
):
    ends, first_steps, all_steps = schedule(list_ref)
    given = [list_ref, source_ref, target_ref, value_ref, exponent_ref, weight_ref, sum_ref]
    totals = Totals(ends, own_blocks, list_ref.shape[0] - 1, given)
    sum_ref[...] = own_sum_ref[...]
    totals.steps(first_steps, all_steps)
    totals.finish(0, out_ref)


def last_totals(lists, sources, targets, values, own_sum, exponent):
    own_blocks = targets.shape[0] // lists.shape[0]
    lists = pltpu.with_memory_space_constraint(lists, pltpu.SMEM)
    total, _ = pl.pallas_call(
        functools.partial(last_totals_kernel, own_blocks),
        out_shape=[
            jax.ShapeDtypeStruct((3, own_blocks, BLOCK), f32),
            pltpu.VMEM(exponent.shape, f32),
        ],
        in_specs=[smem()] + [vmem()] * 5,
        out_specs=[vmem()] * 2,
        scratch_shapes=[
            pltpu.VMEM((own_blocks * 8, BLOCK), f32),
            pltpu.VMEM((STEP, 2 * BLOCK, 2 * BLOCK), bf16),
        ],
        input_output_aliases={5: 1},
        compiler_params=params(14),
        cost_estimate=lasting(8),
        name="last_totals",
    )(lists, *held(sources, targets, values, own_sum, exponent))
    return total


def smoothed_kernel(*refs):
    *parts, out_ref = refs
    totals = [sum(part[r] for part in parts) for r in range(3)]
    for k in range(2):
        ratio = totals[k + 1] / totals[0]
        for t in range(ratio.shape[0]):
            out_ref[k : k + 1, t * BLOCK : (t + 1) * BLOCK] = ratio[t : t + 1]


def smoothed(parts):
    return pl.pallas_call(
        smoothed_kernel,
        out_shape=jax.ShapeDtypeStruct((2, parts[0].shape[1] * BLOCK), f32),
        in_specs=[vmem()] * len(parts),
        out_specs=vmem(),
        compiler_params=params(4),
        cost_estimate=lasting(0.2),
        name="smoothed",
    )(*parts)


def local(partials, coords, volume, send_blocks, halo_counts, source_slots, source_counts):
    cut_count = lax.axis_size("cuts")
    event_count = lax.axis_size("event")
    block_total = volume.shape[0] // BLOCK
    own_blocks = source_slots.shape[2]
    grid_step = cut_count // 4
    my_event = lax.axis_index("event")

    strides = [(1, [[0], [1]])]
    if grid_step == 1:
        strides = [(1, [[0, 2], [1, 3]])]
    else:
        strides.append((grid_step, [[2], [3]]))
    event = my_event.reshape(1)
    mine = partials[0]
    near_coords, near_volume, near_mine, own_list, *parcels = prepare(
        strides, send_blocks.shape[3], event, lax.axis_index("cuts").reshape(1), halo_counts[0],
        source_slots[0, 0].T, source_counts[0], coords, volume.reshape(block_total, BLOCK),
        mine,
    )
    turns = [(stride, turn) for stride, _ in strides for turn in (1, 0)]
    if event_count == 4:
        part, *parcels = half_sum(event, near_mine, crossed(mine, "event", 1), parcels)
        far_part = crossed(part, "event", 2)
    arrived = [swapped(p, *turn) for p, turn in zip(parcels, turns)]
    sources, targets, mark = own_features(event, near_coords, near_volume, own_blocks)
    if event_count == 4:
        part = added(part, far_part, mark)
        summed = [event, part, crossed(part, "event", 1)]
    else:
        summed = [lax.psum(mine, "event")]

    targets, lists = halo_features(
        own_list, targets, send_blocks[0, 0], arrived, block_total
    )
    *halo_totals, own_sum, values, exponent = first_totals(
        lists, sources, targets, summed, block_total
    )
    returned = [swapped(t, *turn) for t, turn in zip(halo_totals, turns)]
    totals = last_totals(lists, sources, targets, values, own_sum, exponent)
    return smoothed([totals, *returned])


def solution(mesh):
    placed = (
        P("event", None, ("runs", "cuts")),
        P(None, ("runs", "cuts")),
        P(("runs", "cuts")),
        P(("runs", "cuts"), "event", None, None),
        P(("runs", "cuts"), "event", None),
        P(("runs", "cuts"), "event", None, None),
        P(("runs", "cuts"), "event", None),
    )
    return jax.shard_map(
        local,
        mesh=mesh,
        in_specs=placed,
        out_specs=P(None, ("runs", "cuts", "event")),
        check_vma=False,
    )
```
